512 devices in a mesh: ctx: 64 (over y, z), head: 8 (over x, core).
Axes of the slice: x: 4, y: 4, z: 16, core: 2. Of those that a mesh axis runs over, the one named last changes fastest.
Arguments:
- queries: bfloat16 [32768, 4096], P(('ctx', 'head')), may hold values from -0.0029296875 to 0.0029296875
- keys: bfloat16 [32768, 4096], P(('ctx', 'head')), may hold values from -0.0029296875 to 0.0029296875
- values: bfloat16 [32768, 4096], P(('ctx', 'head')), may hold values from -6 to 6
- grad_out: bfloat16 [32768, 4096], P(('ctx', 'head')), may hold values from -6 to 6
Outputs:
- grad_queries: bfloat16 [32768, 4096], P(('ctx', 'head'))
- grad_keys: bfloat16 [32768, 4096], P(('ctx', 'head'))
- grad_values: bfloat16 [32768, 4096], P(('ctx', 'head'))
The draws below stay inside these ranges and needn't reach their ends.
All inputs are finite; a program needn't handle non-finite values.
Results may differ from the reference program's by a relative error of at most 0.005.
Values may be sent and summed in bfloat16 or wider, within the bound.
No kernel may reach another device: no remote copies, remote signals or barrier semaphores. Data moves between devices by JAX's collectives and lax.ppermute only.
A program may use at most 128 MiB of HBM per device.

```python
import jax
import jax.numpy as jnp
from jax import lax

D = 4096
HEADS = 32
HEAD_DIM = 128
TOK_CTX = 512
TOKENS = 32768
N_CTX = 64


def steps_of(own_key, dims, split, least, top_value):
    level = 1.0
    for axis_at, shards_of in split:
        heights = jax.random.uniform(jax.random.fold_in(jax.random.fold_in(own_key, 6), axis_at), (shards_of,), jnp.float32, least / len(split), top_value / len(split))
        level = level * jnp.repeat(jnp.exp(heights), dims[axis_at] // shards_of).reshape((-1,) + (1,) * (len(dims) - 1 - axis_at))
    return level


def scatter_about(stream_key, dims, scale, limit, cuts=(), held_as=jnp.bfloat16):
    loudness = steps_of(stream_key, dims, cuts, -0.22, 0.18) if cuts else 1.0
    result = jax.random.normal(stream_key, dims, jnp.float32) * scale * loudness
    return jnp.minimum(jnp.maximum(result, -limit), limit).astype(held_as)


def setup_inputs(seed: int = 0) -> dict:
    key_list = jax.random.split(jax.random.key(seed), 5)
    queries = scatter_about(key_list[0], (TOKENS, D), (TOKENS * HEAD_DIM) ** -0.5, 0.0029296875, ((0, 512),))
    keys = scatter_about(key_list[1], (TOKENS, D), (TOKENS * HEAD_DIM) ** -0.5, 0.0029296875, ((0, 512),))
    values = scatter_about(key_list[2], (TOKENS, D), 1.0, 6.0, ((0, 512),))
    grad_out = scatter_about(key_list[3], (TOKENS, D), 1.0, 6.0, ((0, 512),))
    return {"queries": queries, "keys": keys, "values": values, "grad_out": grad_out}


def one_head(pieces):
    query_h, key_h, value_h, grad_h = [p.astype(jnp.float32) for p in pieces]
    span_state = jnp.einsum("cli,clj->cij", key_h, value_h)
    span_adjoint = jnp.einsum("cli,clj->cij", query_h, grad_h)
    zero_block = jnp.zeros_like(span_state[:1])
    prior_state = jnp.concatenate([zero_block, jnp.cumsum(span_state, axis=0)[:-1]], axis=0)
    reversed_sum = jnp.cumsum(span_adjoint[::-1], axis=0)[::-1]
    later_adjoint = jnp.concatenate([reversed_sum[1:], zero_block], axis=0)
    prior_low = prior_state.astype(jnp.bfloat16).astype(jnp.float32)
    later_low = later_adjoint.astype(jnp.bfloat16).astype(jnp.float32)
    length = query_h.shape[1]
    lower = jnp.arange(length)[:, None] >= jnp.arange(length)[None, :]
    value_scores = jnp.einsum("ctj,csj->cts", grad_h, value_h)
    value_scores = jnp.where(lower[None], value_scores, 0.0).astype(jnp.bfloat16).astype(jnp.float32)
    key_scores = jnp.einsum("cti,csi->cts", query_h, key_h)
    key_scores = jnp.where(lower[None], key_scores, 0.0).astype(jnp.bfloat16).astype(jnp.float32)
    grad_query = jnp.einsum("cts,csi->cti", value_scores, key_h) + jnp.einsum("ctj,cij->cti", grad_h, prior_low)
    grad_key = jnp.einsum("cts,cti->csi", value_scores, query_h) + jnp.einsum("csj,cij->csi", value_h, later_low)
    grad_value = jnp.einsum("cts,ctj->csj", key_scores, grad_h) + jnp.einsum("csi,cij->csj", key_h, later_low)
    return (grad_query.astype(jnp.bfloat16), grad_key.astype(jnp.bfloat16), grad_value.astype(jnp.bfloat16))


def heads_first(array):
    return jnp.moveaxis(array.reshape(N_CTX, TOK_CTX, HEADS, HEAD_DIM), 2, 0)


def rows_back(array):
    return jnp.moveaxis(array, 0, 2).reshape(N_CTX * TOK_CTX, HEADS * HEAD_DIM)


def reference(queries, keys, values, grad_out):
    stacked = (heads_first(queries), heads_first(keys), heads_first(values), heads_first(grad_out))
    grad_query, grad_key, grad_value = lax.map(one_head, stacked)
    return (rows_back(grad_query), rows_back(grad_key), rows_back(grad_value))
```

```python
import functools

import jax
import jax.numpy as jnp
from jax import lax
from jax.experimental import pallas as pl
from jax.experimental.pallas import tpu as pltpu
from jax.sharding import Mesh
from jax.sharding import PartitionSpec as P

HEADS = 32
HEAD_DIM = 128
CORES, NEAR, FAR = 2, 8, 32
HALF_HEADS = HEADS // CORES
OWNED = HALF_HEADS // NEAR
STEPS = 4
STEP_HEADS = HALF_HEADS // STEPS
F32, BF16 = jnp.float32, jnp.bfloat16
VMEM_LIMIT = 40 * 1024 * 1024


def params(**kwargs):
    return pltpu.CompilerParams(vmem_limit_bytes=VMEM_LIMIT, **kwargs)


def dot(a, b, contract):
    return lax.dot_general(a, b, (((contract[0],), (contract[1],)), ((), ())), preferred_element_type=F32)


def pick_kernel(core_ref, q_ref, k_ref, v_ref, g_ref, out_ref, sems):
    half = out_ref.shape[2]
    first = pl.multiple_of((1 - core_ref[0]) * half, half)
    copies = [
        pltpu.make_async_copy(ref.at[:, pl.ds(first, half)], out_ref.at[i], sems.at[i])
        for i, ref in enumerate((q_ref, k_ref, v_ref, g_ref))
    ]
    for copy in copies:
        copy.start()
    for copy in copies:
        copy.wait()


def pick(core, arrays):
    rows, width = arrays[0].shape
    any_space = pl.BlockSpec(memory_space=pl.ANY)
    return pl.pallas_call(
        pick_kernel,
        out_shape=jax.ShapeDtypeStruct((4, rows, width // CORES), BF16),
        in_specs=[pl.BlockSpec(memory_space=pltpu.SMEM)] + [any_space] * 4,
        out_specs=any_space,
        scratch_shapes=[pltpu.SemaphoreType.DMA((4,))],
        compiler_params=params(),
        name="pick_half",
    )(core, *arrays)


def tokens_of(refs, other_ref, head):
    columns = slice(head * HEAD_DIM, (head + 1) * HEAD_DIM)
    return [
        jnp.concatenate([ref[:, columns], other_ref[i, :, columns]], axis=0) for i, ref in enumerate(refs)
    ]


def state_kernel(core_ref, q_ref, k_ref, v_ref, g_ref, other_ref, out_ref):
    for head in range(STEP_HEADS):
        query, key, value, grad = tokens_of((q_ref, k_ref, v_ref, g_ref), other_ref, head)
        out_ref[head // OWNED, 0, head % OWNED] = dot(key, value, (0, 0)).astype(BF16)
        out_ref[head // OWNED, 1, head % OWNED] = dot(query, grad, (0, 0)).astype(BF16)


def token_specs(rows):
    columns = STEP_HEADS * HEAD_DIM
    own = pl.BlockSpec((rows, columns), lambda i, core: (0, core[0] * STEPS + i))
    other = pl.BlockSpec((4, rows, columns), lambda i, core: (0, 0, i))
    state = pl.BlockSpec((STEP_HEADS // OWNED, 2, OWNED, HEAD_DIM, HEAD_DIM), lambda i, core: (i, 0, 0, 0, 0))
    return own, other, state


def chunk_states(core, arrays, other):
    rows = arrays[0].shape[0]
    own_spec, other_spec, state_spec = token_specs(rows)
    return pl.pallas_call(
        state_kernel,
        out_shape=jax.ShapeDtypeStruct((NEAR, 2, OWNED, HEAD_DIM, HEAD_DIM), BF16),
        grid_spec=pltpu.PrefetchScalarGridSpec(
            num_scalar_prefetch=1,
            grid=(STEPS,),
            in_specs=[own_spec] * 4 + [other_spec],
            out_specs=state_spec,
        ),
        compiler_params=params(),
        name="chunk_states",
    )(core, *arrays, other)


def total_kernel(near_ref, out_ref):
    total = near_ref[0].astype(F32)
    for chip in range(1, NEAR):
        total += near_ref[chip].astype(F32)
    out_ref[...] = total.astype(BF16)


def group_total(near):
    return pl.pallas_call(
        total_kernel,
        out_shape=jax.ShapeDtypeStruct(near.shape[1:], BF16),
        compiler_params=params(),
        name="group_total",
    )(near)


def carry_kernel(place_ref, far_ref, out_ref):
    @pl.when(place_ref[0] < FAR // 2)
    def _():
        total = jnp.zeros(far_ref.shape[1:], F32)
        for group in range(FAR):
            out_ref[group] = total.astype(BF16)
            total += far_ref[group].astype(F32)

    @pl.when(place_ref[0] >= FAR // 2)
    def _():
        total = jnp.zeros(far_ref.shape[1:], F32)
        for group in reversed(range(FAR)):
            out_ref[group] = total.astype(BF16)
            total += far_ref[group].astype(F32)


def group_carry(place, far):
    return pl.pallas_call(
        carry_kernel,
        out_shape=jax.ShapeDtypeStruct(far.shape, BF16),
        in_specs=[pl.BlockSpec(memory_space=pltpu.SMEM), pl.BlockSpec(memory_space=pltpu.VMEM)],
        out_specs=pl.BlockSpec(memory_space=pltpu.VMEM),
        compiler_params=params(),
        name="group_carry",
    )(place, far)


def spread_kernel(near_ref, carry_ref, out_ref):
    for head in range(OWNED):
        total = carry_ref[0, head].astype(F32)
        for chip in range(NEAR):
            out_ref[chip, 0, head] = total.astype(BF16)
            total += near_ref[chip, 0, head].astype(F32)
        total = carry_ref[1, head].astype(F32)
        for chip in reversed(range(NEAR)):
            out_ref[chip, 1, head] = total.astype(BF16)
            total += near_ref[chip, 1, head].astype(F32)


def chip_carry(near, carry):
    return pl.pallas_call(
        spread_kernel,
        out_shape=jax.ShapeDtypeStruct(near.shape, BF16),
        compiler_params=params(),
        name="chip_carry",
    )(near, carry)


def grad_kernel(core_ref, q_ref, k_ref, v_ref, g_ref, other_ref, carry_ref, gq_ref, gk_ref, gv_ref, send_ref):
    rows = q_ref.shape[0]
    core = core_ref[0]

    def place(axis):
        at = lax.broadcasted_iota(jnp.int32, (2 * rows, 2 * rows), axis)
        return jnp.where(at < rows, at + core * rows, at - core * rows)

    lower = place(0) >= place(1)
    for head in range(STEP_HEADS):
        query, key, value, grad = tokens_of((q_ref, k_ref, v_ref, g_ref), other_ref, head)
        prior = carry_ref[head // OWNED, 0, head % OWNED]
        later = carry_ref[head // OWNED, 1, head % OWNED]
        value_scores = jnp.where(lower, dot(grad, value, (1, 1)), 0.0).astype(BF16)
        key_scores = jnp.where(lower, dot(query, key, (1, 1)), 0.0).astype(BF16)
        grads = (
            dot(value_scores, key, (1, 0)) + dot(grad, prior, (1, 1)),
            dot(value_scores, query, (0, 0)) + dot(value, later, (1, 1)),
            dot(key_scores, grad, (0, 0)) + dot(key, later, (1, 0)),
        )
        columns = slice(head * HEAD_DIM, (head + 1) * HEAD_DIM)
        for i, (out_ref, result) in enumerate(zip((gq_ref, gk_ref, gv_ref), grads)):
            result = result.astype(BF16)
            out_ref[:, columns] = result[:rows]
            send_ref[i, :, columns] = result[rows:]


def gradients(core, arrays, other, carry):
    rows, width = arrays[0].shape
    own_spec, other_spec, state_spec = token_specs(rows)
    columns = STEP_HEADS * HEAD_DIM
    return pl.pallas_call(
        grad_kernel,
        out_shape=[jax.ShapeDtypeStruct((rows, width), BF16)] * 3
        + [jax.ShapeDtypeStruct((3, rows, width // CORES), BF16)],
        grid_spec=pltpu.PrefetchScalarGridSpec(
            num_scalar_prefetch=1,
            grid=(STEPS,),
            in_specs=[own_spec] * 4 + [other_spec, state_spec],
            out_specs=[own_spec] * 3 + [pl.BlockSpec((3, rows, columns), lambda i, core: (0, 0, i))],
        ),
        compiler_params=params(),
        name="gradients",
    )(core, *arrays, other, carry)


def place_kernel(core_ref, got_ref, q_in, k_in, v_in, gq_ref, gk_ref, gv_ref, sems):
    half = got_ref.shape[2]
    first = pl.multiple_of((1 - core_ref[0]) * half, half)
    copies = [
        pltpu.make_async_copy(got_ref.at[i], ref.at[:, pl.ds(first, half)], sems.at[i])
        for i, ref in enumerate((gq_ref, gk_ref, gv_ref))
    ]
    for copy in copies:
        copy.start()
    for copy in copies:
        copy.wait()


def place_half(core, got, grads):
    any_space = pl.BlockSpec(memory_space=pl.ANY)
    return pl.pallas_call(
        place_kernel,
        out_shape=[jax.ShapeDtypeStruct(array.shape, array.dtype) for array in grads],
        in_specs=[pl.BlockSpec(memory_space=pltpu.SMEM)] + [any_space] * 4,
        out_specs=[any_space] * 3,
        scratch_shapes=[pltpu.SemaphoreType.DMA((3,))],
        input_output_aliases={2: 0, 3: 1, 4: 2},
        compiler_params=params(),
        name="place_half",
    )(core, got, *grads)


def exchange(array, axes):
    return lax.all_to_all(array, axes, split_axis=0, concat_axis=0, tiled=True)


def local(queries, keys, values, grad_out):
    arrays = (queries, keys, values, grad_out)
    near_axes, far_axes = ("zl", "x"), ("y", "zh")
    swap = [(0, 1), (1, 0)]
    core = lax.axis_index("core").reshape(1)
    place = lax.axis_index(far_axes).reshape(1)
    other = lax.ppermute(pick(core, arrays), "core", swap)
    near = exchange(chunk_states(core, arrays, other), near_axes)
    total = group_total(near)
    far = exchange(total.reshape(FAR, -1, HEAD_DIM), far_axes)
    carry = exchange(group_carry(place, far), far_axes).reshape(total.shape)
    carry = exchange(chip_carry(near, carry), near_axes)
    *grads, send = gradients(core, arrays, other, carry)
    return tuple(place_half(core, lax.ppermute(send, "core", swap), grads))


def solution(mesh):
    devices = mesh.devices.reshape(4, 8, 2, 4, 2)
    chips = Mesh(devices, ("y", "zh", "zl", "x", "core"))
    rows = P(("y", "zh", "zl", "x", "core"), None)
    return jax.shard_map(
        local, mesh=chips, in_specs=(rows,) * 4, out_specs=(rows,) * 3, check_vma=False
    )
```

```python
import functools

import jax
import jax.numpy as jnp
from jax import lax
from jax.experimental import pallas as pl
from jax.experimental.pallas import tpu as pltpu
from jax.sharding import Mesh
from jax.sharding import PartitionSpec as P

HEADS = 32
HEAD_DIM = 128
CORES, NEAR, FAR = 2, 8, 32
HALF_HEADS = HEADS // CORES
OWNED = HALF_HEADS // NEAR
STEPS = 4
STEP_HEADS = HALF_HEADS // STEPS
F32, BF16 = jnp.float32, jnp.bfloat16
NEAR_AXES, FAR_AXES = ("zl", "x"), ("y", "zh")
BAND = 16
SMALL, LARGE = 32 * 1024 * 1024, 60 * 1024 * 1024


def params(limit=SMALL):
    return pltpu.CompilerParams(vmem_limit_bytes=limit)


def in_hbm(array):
    return pltpu.with_memory_space_constraint(array, pltpu.HBM)


def dot(a, b, contract):
    return lax.dot_general(a, b, (((contract[0],), (contract[1],)), ((), ())), preferred_element_type=F32)


def copy_all(pairs, sems):
    copies = []
    for source, target in pairs:
        for first in range(0, source.shape[0], BAND):
            band = pl.ds(first, BAND)
            copies.append(pltpu.make_async_copy(source.at[band], target.at[band], sems.at[len(copies)]))
    for copy in copies:
        copy.start()
    for copy in copies:
        copy.wait()


def pick_kernel(own, q_ref, k_ref, v_ref, g_ref, out_ref, sems):
    half = out_ref.shape[2]
    core = lax.axis_index("core")
    columns = pl.ds(pl.multiple_of((core if own else 1 - core) * half, half), half)
    copy_all([(ref.at[:, columns], out_ref.at[i]) for i, ref in enumerate((q_ref, k_ref, v_ref, g_ref))], sems)


def pick(arrays, own):
    rows, width = arrays[0].shape
    return pl.pallas_call(
        functools.partial(pick_kernel, own),
        out_shape=pltpu.VMEM((4, rows, width // CORES), BF16),
        in_specs=[pl.BlockSpec(memory_space=pltpu.HBM)] * 4,
        out_specs=pl.BlockSpec(memory_space=pltpu.VMEM),
        scratch_shapes=[pltpu.SemaphoreType.DMA((4 * rows // BAND,))],
        compiler_params=params(),
        cost_estimate=pl.CostEstimate(flops=0, bytes_accessed=2 * 4 * rows * width, transcendentals=0),
        name="own_half" if own else "other_half",
    )(*[in_hbm(array) for array in arrays])


def state_kernel(own_ref, other_ref, out_ref, held, sems):
    copies = []
    for owner in range(NEAR):
        for head in range(OWNED):
            first = (owner * OWNED + head) * HEAD_DIM
            columns = slice(first, first + HEAD_DIM)
            query, key, value, grad = [
                jnp.concatenate([own_ref[i, :, columns], other_ref[i, :, columns]], axis=0) for i in range(4)
            ]
            held[owner, 0, head] = dot(key, value, (0, 0)).astype(BF16)
            held[owner, 1, head] = dot(query, grad, (0, 0)).astype(BF16)
        copies.append(pltpu.make_async_copy(held.at[owner], out_ref.at[owner], sems.at[owner]))
        copies[-1].start()
    for copy in copies:
        copy.wait()


def chunk_states(own, other):
    shape = (NEAR, 2, OWNED, HEAD_DIM, HEAD_DIM)
    return pl.pallas_call(
        state_kernel,
        out_shape=pltpu.HBM(shape, BF16),
        in_specs=[pl.BlockSpec(memory_space=pltpu.VMEM)] * 2,
        out_specs=pl.BlockSpec(memory_space=pltpu.HBM),
        scratch_shapes=[pltpu.VMEM(shape, BF16), pltpu.SemaphoreType.DMA((NEAR,))],
        compiler_params=params(),
        name="chunk_states",
    )(own, other)


def tokens_of(refs, other_ref, head):
    columns = slice(head * HEAD_DIM, (head + 1) * HEAD_DIM)
    return [
        jnp.concatenate([ref[:, columns], other_ref[i, :, columns]], axis=0) for i, ref in enumerate(refs)
    ]


def token_specs(rows):
    columns = STEP_HEADS * HEAD_DIM
    own = pl.BlockSpec((rows, columns), lambda i, core: (0, core[0] * STEPS + i))
    other = pl.BlockSpec((4, rows, columns), lambda i, core: (0, 0, i))
    state = pl.BlockSpec((STEP_HEADS // OWNED, 2, OWNED, HEAD_DIM, HEAD_DIM), lambda i, core: (i, 0, 0, 0, 0))
    return own, other, state


def total_kernel(near_ref, out_ref):
    total = near_ref[0].astype(F32)
    for chip in range(1, NEAR):
        total += near_ref[chip].astype(F32)
    out_ref[...] = total.astype(BF16)


def group_total(near):
    return pl.pallas_call(
        total_kernel,
        out_shape=jax.ShapeDtypeStruct(near.shape[1:], BF16),
        in_specs=[pl.BlockSpec(memory_space=pltpu.VMEM)],
        out_specs=pl.BlockSpec(memory_space=pltpu.VMEM),
        compiler_params=params(),
        name="group_total",
    )(near)


def carry_kernel(far_ref, out_ref):
    place = lax.axis_index(FAR_AXES)

    @pl.when(place < FAR // 2)
    def _():
        total = jnp.zeros(far_ref.shape[1:], F32)
        for group in range(FAR):
            out_ref[group] = total.astype(BF16)
            total += far_ref[group].astype(F32)

    @pl.when(place >= FAR // 2)
    def _():
        total = jnp.zeros(far_ref.shape[1:], F32)
        for group in reversed(range(FAR)):
            out_ref[group] = total.astype(BF16)
            total += far_ref[group].astype(F32)


def group_carry(far):
    return pl.pallas_call(
        carry_kernel,
        out_shape=jax.ShapeDtypeStruct(far.shape, BF16),
        in_specs=[pl.BlockSpec(memory_space=pltpu.VMEM)],
        out_specs=pl.BlockSpec(memory_space=pltpu.VMEM),
        compiler_params=params(),
        name="group_carry",
    )(far)


def spread_kernel(near_ref, carry_ref, out_ref):
    for head in range(OWNED):
        total = carry_ref[0, head].astype(F32)
        for chip in range(NEAR):
            out_ref[chip, 0, head] = total.astype(BF16)
            total += near_ref[chip, 0, head].astype(F32)
        total = carry_ref[1, head].astype(F32)
        for chip in reversed(range(NEAR)):
            out_ref[chip, 1, head] = total.astype(BF16)
            total += near_ref[chip, 1, head].astype(F32)


def chip_carry(near, carry):
    return pl.pallas_call(
        spread_kernel,
        out_shape=jax.ShapeDtypeStruct(near.shape, BF16),
        in_specs=[pl.BlockSpec(memory_space=pltpu.VMEM)] * 2,
        out_specs=pl.BlockSpec(memory_space=pltpu.VMEM),
        compiler_params=params(),
        name="chip_carry",
    )(near, carry)


def inner_kernel(core_ref, q_ref, k_ref, v_ref, g_ref, other_ref, out_ref, kept_ref):
    rows = q_ref.shape[0]
    core = core_ref[0]

    def place(axis):
        at = lax.broadcasted_iota(jnp.int32, (2 * rows, 2 * rows), axis)
        return jnp.where(at < rows, at + core * rows, at - core * rows)

    lower = place(0) >= place(1)
    for head in range(STEP_HEADS):
        query, key, value, grad = tokens_of((q_ref, k_ref, v_ref, g_ref), other_ref, head)
        value_scores = jnp.where(lower, dot(grad, value, (1, 1)), 0.0).astype(BF16)
        key_scores = jnp.where(lower, dot(query, key, (1, 1)), 0.0).astype(BF16)
        columns = slice(head * HEAD_DIM, (head + 1) * HEAD_DIM)
        out_ref[0, :, columns] = dot(value_scores, key, (1, 0))
        out_ref[1, :, columns] = dot(value_scores, query, (0, 0))
        out_ref[2, :, columns] = dot(key_scores, grad, (0, 0))
        for i, operand in enumerate((grad, value, key)):
            kept_ref[i, :, columns] = operand


def inner_part(core, arrays, other):
    rows, width = arrays[0].shape
    own_spec, other_spec, _ = token_specs(rows)
    columns = STEP_HEADS * HEAD_DIM
    return pl.pallas_call(
        inner_kernel,
        out_shape=[pltpu.HBM((3, 2 * rows, width // CORES), dtype) for dtype in (F32, BF16)],
        grid_spec=pltpu.PrefetchScalarGridSpec(
            num_scalar_prefetch=1,
            grid=(STEPS,),
            in_specs=[own_spec] * 4 + [other_spec],
            out_specs=[pl.BlockSpec((3, 2 * rows, columns), lambda i, core: (0, 0, i))] * 2,
        ),
        compiler_params=params(LARGE),
        cost_estimate=pl.CostEstimate(
            flops=10 * HALF_HEADS * (2 * rows) ** 2 * HEAD_DIM, bytes_accessed=12 * 2**20, transcendentals=0
        ),
        name="inner_part",
    )(core, *arrays, other)


def outer_part(rows, head, inner_ref, kept_ref, carry_ref):
    columns = slice(head * HEAD_DIM, (head + 1) * HEAD_DIM)
    grad, value, key = [kept_ref[i, rows, columns] for i in range(3)]
    prior = carry_ref[head // OWNED, 0, head % OWNED]
    later = carry_ref[head // OWNED, 1, head % OWNED]
    outer = (dot(grad, prior, (1, 1)), dot(value, later, (1, 1)), dot(key, later, (1, 0)))
    return columns, [(part + inner_ref[i, rows, columns]).astype(BF16) for i, part in enumerate(outer)]


def other_kernel(inner_ref, kept_ref, carry_ref, out_ref):
    rows = out_ref.shape[1]
    for head in range(HALF_HEADS):
        columns, results = outer_part(slice(rows, 2 * rows), head, inner_ref, kept_ref, carry_ref)
        for i, result in enumerate(results):
            out_ref[i, :, columns] = result


def other_gradients(inner, kept, carry):
    _, rows, half = kept.shape
    return pl.pallas_call(
        other_kernel,
        out_shape=pltpu.VMEM((3, rows // 2, half), BF16),
        in_specs=[pl.BlockSpec(memory_space=pltpu.VMEM)] * 3,
        out_specs=pl.BlockSpec(memory_space=pltpu.VMEM),
        compiler_params=params(),
        name="other_gradients",
    )(inner, kept, carry)


def own_kernel(inner_ref, kept_ref, carry_ref, gq_ref, gk_ref, gv_ref, held, sems):
    rows, half = held.shape[1:]
    place = lax.axis_index("core") * half
    copies = []
    for head in range(HALF_HEADS):
        columns, results = outer_part(slice(0, rows), head, inner_ref, kept_ref, carry_ref)
        for i, result in enumerate(results):
            held[i, :, columns] = result
        if (head + 1) % STEP_HEADS == 0:
            width = STEP_HEADS * HEAD_DIM
            first = columns.stop - width
            for i, ref in enumerate((gq_ref, gk_ref, gv_ref)):
                target = ref.at[:, pl.ds(pl.multiple_of(place + first, width), width)]
                copies.append(
                    pltpu.make_async_copy(held.at[i, :, pl.ds(first, width)], target, sems.at[len(copies)])
                )
                copies[-1].start()
    for copy in copies:
        copy.wait()


def own_gradients(inner, kept, carry):
    _, rows, half = kept.shape
    return pl.pallas_call(
        own_kernel,
        out_shape=[pltpu.HBM((rows // 2, half * CORES), BF16)] * 3,
        in_specs=[pl.BlockSpec(memory_space=pltpu.VMEM)] * 3,
        out_specs=[pl.BlockSpec(memory_space=pltpu.HBM)] * 3,
        scratch_shapes=[pltpu.VMEM((3, rows // 2, half), BF16), pltpu.SemaphoreType.DMA((3 * STEPS,))],
        compiler_params=params(),
        cost_estimate=pl.CostEstimate(
            flops=3 * HALF_HEADS * rows * HEAD_DIM**2, bytes_accessed=4 * 2**20, transcendentals=0
        ),
        name="own_gradients",
    )(inner, kept, carry)


def place_kernel(got_ref, q_in, k_in, v_in, gq_ref, gk_ref, gv_ref, sems):
    half = got_ref.shape[2]
    columns = pl.ds(pl.multiple_of((1 - lax.axis_index("core")) * half, half), half)
    copy_all([(got_ref.at[i], ref.at[:, columns]) for i, ref in enumerate((gq_ref, gk_ref, gv_ref))], sems)


def place_half(got, grads):
    any_space = pl.BlockSpec(memory_space=pl.ANY)
    return pl.pallas_call(
        place_kernel,
        out_shape=[jax.ShapeDtypeStruct(array.shape, array.dtype) for array in grads],
        in_specs=[pl.BlockSpec(memory_space=pltpu.VMEM)] + [any_space] * 3,
        out_specs=[any_space] * 3,
        scratch_shapes=[pltpu.SemaphoreType.DMA((3 * got.shape[1] // BAND,))],
        input_output_aliases={1: 0, 2: 1, 3: 2},
        compiler_params=params(),
        name="place_half",
    )(got, *grads)


def exchange(array, axes):
    return lax.all_to_all(array, axes, split_axis=0, concat_axis=0, tiled=True)


def local(queries, keys, values, grad_out):
    arrays = (queries, keys, values, grad_out)
    swap = [(0, 1), (1, 0)]
    core = lax.axis_index("core").reshape(1)
    other = lax.ppermute(pick(arrays, False), "core", swap)
    near = exchange(chunk_states(pick(arrays, True), other), NEAR_AXES)
    near, *inner = lax.optimization_barrier((near, *inner_part(core, arrays, other)))
    total = group_total(near)
    far = exchange(total.reshape(FAR, -1, HEAD_DIM), FAR_AXES)
    carry = exchange(group_carry(far), FAR_AXES).reshape(total.shape)
    carry = exchange(chip_carry(near, carry), NEAR_AXES)
    got = lax.ppermute(other_gradients(*inner, carry), "core", swap)
    return tuple(place_half(got, own_gradients(*inner, carry)))


def solution(mesh):
    devices = mesh.devices.reshape(4, 8, 2, 4, 2)
    chips = Mesh(devices, ("y", "zh", "zl", "x", "core"))
    rows = P(("y", "zh", "zl", "x", "core"), None)
    return jax.shard_map(
        local, mesh=chips, in_specs=(rows,) * 4, out_specs=(rows,) * 3, check_vma=False
    )
```

```python
import functools

import jax
import jax.numpy as jnp
from jax import lax
from jax.experimental import pallas as pl
from jax.experimental.pallas import tpu as pltpu
from jax.sharding import Mesh
from jax.sharding import PartitionSpec as P

HEADS = 32
HEAD_DIM = 128
CORES, NEAR, FAR = 2, 8, 32
HALF_HEADS = HEADS // CORES
OWNED = HALF_HEADS // NEAR
STEPS = 4
STEP_HEADS = HALF_HEADS // STEPS
F32, BF16 = jnp.float32, jnp.bfloat16
NEAR_AXES, FAR_AXES = ("zl", "x"), ("y", "zh")
BAND = 64
SMALL, LARGE = 32 * 1024 * 1024, 60 * 1024 * 1024


def params(limit=SMALL):
    return pltpu.CompilerParams(vmem_limit_bytes=limit)


def in_hbm(array):
    return pltpu.with_memory_space_constraint(array, pltpu.HBM)


def dot(a, b, contract):
    return lax.dot_general(a, b, (((contract[0],), (contract[1],)), ((), ())), preferred_element_type=F32)


def copy_all(pairs, sems):
    copies = []
    for source, target in pairs:
        for first in range(0, source.shape[0], BAND):
            band = pl.ds(first, BAND)
            copies.append(pltpu.make_async_copy(source.at[band], target.at[band], sems.at[len(copies)]))
    for copy in copies:
        copy.start()
    for copy in copies:
        copy.wait()


def pick_kernel(own, q_ref, k_ref, v_ref, g_ref, out_ref, sems):
    half = out_ref.shape[2]
    core = lax.axis_index("core")
    columns = pl.ds(pl.multiple_of((core if own else 1 - core) * half, half), half)
    copy_all([(ref.at[:, columns], out_ref.at[i]) for i, ref in enumerate((q_ref, k_ref, v_ref, g_ref))], sems)


def pick(arrays, own):
    rows, width = arrays[0].shape
    return pl.pallas_call(
        functools.partial(pick_kernel, own),
        out_shape=pltpu.VMEM((4, rows, width // CORES), BF16),
        in_specs=[pl.BlockSpec(memory_space=pltpu.HBM)] * 4,
        out_specs=pl.BlockSpec(memory_space=pltpu.VMEM),
        scratch_shapes=[pltpu.SemaphoreType.DMA((4 * rows // BAND,))],
        compiler_params=params(),
        cost_estimate=pl.CostEstimate(flops=0, bytes_accessed=2 * 4 * rows * width, transcendentals=0),
        name="own_half" if own else "other_half",
    )(*[in_hbm(array) for array in arrays])


def state_kernel(own_ref, other_ref, out_ref, held, sems):
    copies = []
    for owner in range(NEAR):
        for head in range(OWNED):
            first = (owner * OWNED + head) * HEAD_DIM
            columns = slice(first, first + HEAD_DIM)
            query, key, value, grad = [
                jnp.concatenate([own_ref[i, :, columns], other_ref[i, :, columns]], axis=0) for i in range(4)
            ]
            held[owner, 0, head] = dot(key, value, (0, 0)).astype(BF16)
            held[owner, 1, head] = dot(query, grad, (0, 0)).astype(BF16)
        copies.append(pltpu.make_async_copy(held.at[owner], out_ref.at[owner], sems.at[owner]))
        copies[-1].start()
    for copy in copies:
        copy.wait()


def chunk_states(own, other):
    shape = (NEAR, 2, OWNED, HEAD_DIM, HEAD_DIM)
    return pl.pallas_call(
        state_kernel,
        out_shape=pltpu.HBM(shape, BF16),
        in_specs=[pl.BlockSpec(memory_space=pltpu.VMEM)] * 2,
        out_specs=pl.BlockSpec(memory_space=pltpu.HBM),
        scratch_shapes=[pltpu.VMEM(shape, BF16), pltpu.SemaphoreType.DMA((NEAR,))],
        compiler_params=params(),
        name="chunk_states",
    )(own, other)


def tokens_of(refs, other_ref, head):
    columns = slice(head * HEAD_DIM, (head + 1) * HEAD_DIM)
    return [
        jnp.concatenate([ref[:, columns], other_ref[i, :, columns]], axis=0) for i, ref in enumerate(refs)
    ]


def token_specs(rows):
    columns = STEP_HEADS * HEAD_DIM
    own = pl.BlockSpec((rows, columns), lambda i, core: (0, core[0] * STEPS + i))
    other = pl.BlockSpec((4, rows, columns), lambda i, core: (0, 0, i))
    state = pl.BlockSpec((STEP_HEADS // OWNED, 2, OWNED, HEAD_DIM, HEAD_DIM), lambda i, core: (i, 0, 0, 0, 0))
    return own, other, state


def total_kernel(near_ref, out_ref):
    total = near_ref[0].astype(F32)
    for chip in range(1, NEAR):
        total += near_ref[chip].astype(F32)
    out_ref[...] = total.astype(BF16)


def group_total(near):
    return pl.pallas_call(
        total_kernel,
        out_shape=jax.ShapeDtypeStruct(near.shape[1:], BF16),
        in_specs=[pl.BlockSpec(memory_space=pltpu.VMEM)],
        out_specs=pl.BlockSpec(memory_space=pltpu.VMEM),
        compiler_params=params(),
        name="group_total",
    )(near)


def carry_kernel(far_ref, out_ref):
    place = lax.axis_index(FAR_AXES)

    @pl.when(place < FAR // 2)
    def _():
        total = jnp.zeros(far_ref.shape[1:], F32)
        for group in range(FAR):
            out_ref[group] = total.astype(BF16)
            total += far_ref[group].astype(F32)

    @pl.when(place >= FAR // 2)
    def _():
        total = jnp.zeros(far_ref.shape[1:], F32)
        for group in reversed(range(FAR)):
            out_ref[group] = total.astype(BF16)
            total += far_ref[group].astype(F32)


def group_carry(far):
    return pl.pallas_call(
        carry_kernel,
        out_shape=jax.ShapeDtypeStruct(far.shape, BF16),
        in_specs=[pl.BlockSpec(memory_space=pltpu.VMEM)],
        out_specs=pl.BlockSpec(memory_space=pltpu.VMEM),
        compiler_params=params(),
        name="group_carry",
    )(far)


def spread_kernel(near_ref, carry_ref, out_ref):
    for head in range(OWNED):
        total = carry_ref[0, head].astype(F32)
        for chip in range(NEAR):
            out_ref[chip, 0, head] = total.astype(BF16)
            total += near_ref[chip, 0, head].astype(F32)
        total = carry_ref[1, head].astype(F32)
        for chip in reversed(range(NEAR)):
            out_ref[chip, 1, head] = total.astype(BF16)
            total += near_ref[chip, 1, head].astype(F32)


def chip_carry(near, carry):
    return pl.pallas_call(
        spread_kernel,
        out_shape=jax.ShapeDtypeStruct(near.shape, BF16),
        in_specs=[pl.BlockSpec(memory_space=pltpu.VMEM)] * 2,
        out_specs=pl.BlockSpec(memory_space=pltpu.VMEM),
        compiler_params=params(),
        name="chip_carry",
    )(near, carry)


def inner_kernel(core_ref, q_ref, k_ref, v_ref, g_ref, other_ref, out_ref, kept_ref):
    rows = q_ref.shape[0]
    core = core_ref[0]

    def place(axis):
        at = lax.broadcasted_iota(jnp.int32, (2 * rows, 2 * rows), axis)
        return jnp.where(at < rows, at + core * rows, at - core * rows)

    lower = place(0) >= place(1)
    for head in range(STEP_HEADS):
        query, key, value, grad = tokens_of((q_ref, k_ref, v_ref, g_ref), other_ref, head)
        value_scores = jnp.where(lower, dot(grad, value, (1, 1)), 0.0).astype(BF16)
        key_scores = jnp.where(lower, dot(query, key, (1, 1)), 0.0).astype(BF16)
        columns = slice(head * HEAD_DIM, (head + 1) * HEAD_DIM)
        out_ref[0, :, columns] = dot(value_scores, key, (1, 0))
        out_ref[1, :, columns] = dot(value_scores, query, (0, 0))
        out_ref[2, :, columns] = dot(key_scores, grad, (0, 0))
        for i, operand in enumerate((grad, value, key)):
            kept_ref[i, :, columns] = operand


def inner_part(core, arrays, other):
    rows, width = arrays[0].shape
    own_spec, other_spec, _ = token_specs(rows)
    columns = STEP_HEADS * HEAD_DIM
    return pl.pallas_call(
        inner_kernel,
        out_shape=[pltpu.HBM((3, 2 * rows, width // CORES), dtype) for dtype in (F32, BF16)],
        grid_spec=pltpu.PrefetchScalarGridSpec(
            num_scalar_prefetch=1,
            grid=(STEPS,),
            in_specs=[own_spec] * 4 + [other_spec],
            out_specs=[pl.BlockSpec((3, 2 * rows, columns), lambda i, core: (0, 0, i))] * 2,
        ),
        compiler_params=params(LARGE),
        cost_estimate=pl.CostEstimate(
            flops=10 * HALF_HEADS * (2 * rows) ** 2 * HEAD_DIM, bytes_accessed=12 * 2**20, transcendentals=0
        ),
        name="inner_part",
    )(core, *arrays, other)


def outer_part(rows, head, inner_ref, kept_ref, carry_ref):
    columns = slice(head * HEAD_DIM, (head + 1) * HEAD_DIM)
    grad, value, key = [kept_ref[i, rows, columns] for i in range(3)]
    prior = carry_ref[head // OWNED, 0, head % OWNED]
    later = carry_ref[head // OWNED, 1, head % OWNED]
    outer = (dot(grad, prior, (1, 1)), dot(value, later, (1, 1)), dot(key, later, (1, 0)))
    return columns, [(part + inner_ref[i, rows, columns]).astype(BF16) for i, part in enumerate(outer)]


def other_kernel(inner_ref, kept_ref, carry_ref, out_ref):
    rows = out_ref.shape[1]
    for head in range(HALF_HEADS):
        columns, results = outer_part(slice(rows, 2 * rows), head, inner_ref, kept_ref, carry_ref)
        for i, result in enumerate(results):
            out_ref[i, :, columns] = result


def other_gradients(inner, kept, carry):
    _, rows, half = kept.shape
    return pl.pallas_call(
        other_kernel,
        out_shape=pltpu.VMEM((3, rows // 2, half), BF16),
        in_specs=[pl.BlockSpec(memory_space=pltpu.VMEM)] * 3,
        out_specs=pl.BlockSpec(memory_space=pltpu.VMEM),
        compiler_params=params(),
        name="other_gradients",
    )(inner, kept, carry)


def own_kernel(inner_ref, kept_ref, carry_ref, gq_ref, gk_ref, gv_ref, held, sems):
    rows, half = held.shape[1:]
    place = lax.axis_index("core") * half
    copies = []
    for head in range(HALF_HEADS):
        columns, results = outer_part(slice(0, rows), head, inner_ref, kept_ref, carry_ref)
        for i, result in enumerate(results):
            held[i, :, columns] = result
        if (head + 1) % STEP_HEADS == 0:
            width = STEP_HEADS * HEAD_DIM
            first = columns.stop - width
            for i, ref in enumerate((gq_ref, gk_ref, gv_ref)):
                target = ref.at[:, pl.ds(pl.multiple_of(place + first, width), width)]
                copies.append(
                    pltpu.make_async_copy(held.at[i, :, pl.ds(first, width)], target, sems.at[len(copies)])
                )
                copies[-1].start()
    for copy in copies:
        copy.wait()


def own_gradients(inner, kept, carry):
    _, rows, half = kept.shape
    return pl.pallas_call(
        own_kernel,
        out_shape=[pltpu.HBM((rows // 2, half * CORES), BF16)] * 3,
        in_specs=[pl.BlockSpec(memory_space=pltpu.VMEM)] * 3,
        out_specs=[pl.BlockSpec(memory_space=pltpu.HBM)] * 3,
        scratch_shapes=[pltpu.VMEM((3, rows // 2, half), BF16), pltpu.SemaphoreType.DMA((3 * STEPS,))],
        compiler_params=params(),
        cost_estimate=pl.CostEstimate(
            flops=3 * HALF_HEADS * rows * HEAD_DIM**2, bytes_accessed=4 * 2**20, transcendentals=0
        ),
        name="own_gradients",
    )(inner, kept, carry)


def place_kernel(got_ref, q_in, k_in, v_in, gq_ref, gk_ref, gv_ref, sems):
    half = got_ref.shape[2]
    columns = pl.ds(pl.multiple_of((1 - lax.axis_index("core")) * half, half), half)
    copy_all([(got_ref.at[i], ref.at[:, columns]) for i, ref in enumerate((gq_ref, gk_ref, gv_ref))], sems)


def place_half(got, grads):
    any_space = pl.BlockSpec(memory_space=pl.ANY)
    return pl.pallas_call(
        place_kernel,
        out_shape=[jax.ShapeDtypeStruct(array.shape, array.dtype) for array in grads],
        in_specs=[pl.BlockSpec(memory_space=pltpu.VMEM)] + [any_space] * 3,
        out_specs=[any_space] * 3,
        scratch_shapes=[pltpu.SemaphoreType.DMA((3 * got.shape[1] // BAND,))],
        input_output_aliases={1: 0, 2: 1, 3: 2},
        compiler_params=params(),
        name="place_half",
    )(got, *grads)


def exchange(array, axes):
    return lax.all_to_all(array, axes, split_axis=0, concat_axis=0, tiled=True)


def local(queries, keys, values, grad_out):
    arrays = (queries, keys, values, grad_out)
    swap = [(0, 1), (1, 0)]
    core = lax.axis_index("core").reshape(1)
    other = lax.ppermute(pick(arrays, False), "core", swap)
    near = exchange(chunk_states(pick(arrays, True), other), NEAR_AXES)
    near, *inner = lax.optimization_barrier((near, *inner_part(core, arrays, other)))
    total = group_total(near)
    far = exchange(total.reshape(FAR, -1, HEAD_DIM), FAR_AXES)
    carry = exchange(group_carry(far), FAR_AXES).reshape(total.shape)
    carry = exchange(chip_carry(near, carry), NEAR_AXES)
    got = lax.ppermute(other_gradients(*inner, carry), "core", swap)
    return tuple(place_half(got, own_gradients(*inner, carry)))


def solution(mesh):
    devices = mesh.devices.reshape(4, 8, 2, 4, 2)
    chips = Mesh(devices, ("y", "zh", "zl", "x", "core"))
    rows = P(("y", "zh", "zl", "x", "core"), None)
    return jax.shard_map(
        local, mesh=chips, in_specs=(rows,) * 4, out_specs=(rows,) * 3, check_vma=False
    )
```

```python
import functools

import jax
import jax.numpy as jnp
from jax import lax
from jax.experimental import pallas as pl
from jax.experimental.pallas import tpu as pltpu
from jax.sharding import Mesh
from jax.sharding import PartitionSpec as P

HEADS = 32
HEAD_DIM = 128
CORES, SPANS_Y, NEAR_Y, CHIPS, FAR_Z, BLOCK = 2, 4, 4, 8, 8, 16
NEAR, FAR = NEAR_Y * CHIPS, SPANS_Y // NEAR_Y * FAR_Z
HALF_HEADS = HEADS // CORES
OWNED_ROWS = HALF_HEADS * HEAD_DIM // NEAR
STEPS = 4
STEP_HEADS = HALF_HEADS // STEPS
F32, BF16 = jnp.float32, jnp.bfloat16
NEAR_AXES, FAR_AXES = ("yn", "zl", "x"), ("yf", "zh")
BAND = 64
SMALL, LARGE = 32 * 1024 * 1024, 60 * 1024 * 1024


def params(limit=SMALL):
    return pltpu.CompilerParams(vmem_limit_bytes=limit)


def in_hbm(array):
    return pltpu.with_memory_space_constraint(array, pltpu.HBM)


def dot(a, b, contract):
    return lax.dot_general(a, b, (((contract[0],), (contract[1],)), ((), ())), preferred_element_type=F32)


def copy_all(pairs, sems):
    copies = []
    for source, target in pairs:
        for first in range(0, source.shape[0], BAND):
            band = pl.ds(first, BAND)
            copies.append(pltpu.make_async_copy(source.at[band], target.at[band], sems.at[len(copies)]))
    for copy in copies:
        copy.start()
    for copy in copies:
        copy.wait()


def pick_kernel(own, q_ref, k_ref, v_ref, g_ref, out_ref, sems):
    half = out_ref.shape[2]
    core = lax.axis_index("core")
    columns = pl.ds(pl.multiple_of((core if own else 1 - core) * half, half), half)
    copy_all([(ref.at[:, columns], out_ref.at[i]) for i, ref in enumerate((q_ref, k_ref, v_ref, g_ref))], sems)


def pick(arrays, own):
    rows, width = arrays[0].shape
    return pl.pallas_call(
        functools.partial(pick_kernel, own),
        out_shape=pltpu.VMEM((4, rows, width // CORES), BF16),
        in_specs=[pl.BlockSpec(memory_space=pltpu.HBM)] * 4,
        out_specs=pl.BlockSpec(memory_space=pltpu.VMEM),
        scratch_shapes=[pltpu.SemaphoreType.DMA((4 * rows // BAND,))],
        compiler_params=params(),
        cost_estimate=pl.CostEstimate(flops=0, bytes_accessed=2 * 4 * rows * width, transcendentals=0),
        name="own_half" if own else "other_half",
    )(*[in_hbm(array) for array in arrays])


def state_kernel(own_ref, other_ref, out_ref, held, sems):
    copies = []
    for head in range(HALF_HEADS):
        columns = slice(head * HEAD_DIM, (head + 1) * HEAD_DIM)
        query, key, value, grad = [
            jnp.concatenate([own_ref[i, :, columns], other_ref[i, :, columns]], axis=0) for i in range(4)
        ]
        for i, state in enumerate((dot(key, value, (0, 0)), dot(query, grad, (0, 0)))):
            write_state(held, head, i, state.astype(BF16))
        if (head + 1) % 2 == 0:
            share = pl.ds((head - 1) * NEAR // HALF_HEADS, 2 * NEAR // HALF_HEADS)
            copies.append(pltpu.make_async_copy(held.at[share], out_ref.at[share], sems.at[len(copies)]))
            copies[-1].start()
    for copy in copies:
        copy.wait()


def write_state(ref, head, i, state):
    first = head * HEAD_DIM
    for row in range(0, HEAD_DIM, min(HEAD_DIM, OWNED_ROWS)):
        owner, at = divmod(first + row, OWNED_ROWS)
        count = min(HEAD_DIM, OWNED_ROWS)
        ref[owner, i, at : at + count] = state[row : row + count]


def read_state(ref, head, i):
    first, count = head * HEAD_DIM, min(HEAD_DIM, OWNED_ROWS)
    parts = []
    for row in range(0, HEAD_DIM, count):
        owner, at = divmod(first + row, OWNED_ROWS)
        parts.append(ref[owner, i, at : at + count])
    return parts[0] if len(parts) == 1 else jnp.concatenate(parts, axis=0)


def chunk_states(own, other):
    shape = (NEAR, 2, OWNED_ROWS, HEAD_DIM)
    return pl.pallas_call(
        state_kernel,
        out_shape=pltpu.HBM(shape, BF16),
        in_specs=[pl.BlockSpec(memory_space=pltpu.VMEM)] * 2,
        out_specs=pl.BlockSpec(memory_space=pltpu.HBM),
        scratch_shapes=[pltpu.VMEM(shape, BF16), pltpu.SemaphoreType.DMA((HALF_HEADS // 2,))],
        compiler_params=params(),
        name="chunk_states",
    )(own, other)


def tokens_of(refs, other_ref, head):
    columns = slice(head * HEAD_DIM, (head + 1) * HEAD_DIM)
    return [
        jnp.concatenate([ref[:, columns], other_ref[i, :, columns]], axis=0) for i, ref in enumerate(refs)
    ]


def token_specs(rows):
    columns = STEP_HEADS * HEAD_DIM
    own = pl.BlockSpec((rows, columns), lambda i, core: (0, core[0] * STEPS + i))
    other = pl.BlockSpec((4, rows, columns), lambda i, core: (0, 0, i))
    return own, other


def total_kernel(near_ref, out_ref):
    half = FAR // 2
    for span in range(NEAR_Y):
        total = near_ref[span * CHIPS].astype(F32)
        for chip in range(1, CHIPS):
            total += near_ref[span * CHIPS + chip].astype(F32)
        total = total.astype(BF16)
        for slot in range(FAR):
            block = slot % half * BLOCK
            out_ref[slot, span] = total[slot // half, block : block + BLOCK]


def group_total(near):
    return pl.pallas_call(
        total_kernel,
        out_shape=pltpu.VMEM((FAR, NEAR_Y, BLOCK, HEAD_DIM), BF16),
        in_specs=[pl.BlockSpec(memory_space=pltpu.VMEM)],
        out_specs=pl.BlockSpec(memory_space=pltpu.VMEM),
        compiler_params=params(),
        name="group_total",
    )(near)


def groups_in_order():
    order = []
    for y in range(SPANS_Y):
        far_at, near_at = divmod(y, NEAR_Y)
        order += [(far_at * FAR_Z + z, near_at) for z in range(FAR_Z)]
    return order


def carry_kernel(far_ref, out_ref):
    place = lax.axis_index(FAR_AXES)

    def run(order):
        total = jnp.zeros((BLOCK, HEAD_DIM), F32)
        for group in order:
            out_ref[group] = total.astype(BF16)
            total += far_ref[group].astype(F32)

    @pl.when(place < FAR // 2)
    def _():
        run(groups_in_order())

    @pl.when(place >= FAR // 2)
    def _():
        run(groups_in_order()[::-1])


def group_carry(far):
    return pl.pallas_call(
        carry_kernel,
        out_shape=pltpu.VMEM(far.shape, BF16),
        in_specs=[pl.BlockSpec(memory_space=pltpu.VMEM)],
        out_specs=pl.BlockSpec(memory_space=pltpu.VMEM),
        compiler_params=params(),
        name="group_carry",
    )(far)


def spread_kernel(near_ref, carry_ref, out_ref):
    half = FAR // 2
    for span in range(NEAR_Y):
        for i, order in enumerate((range(CHIPS), range(CHIPS)[::-1])):
            total = jnp.concatenate([carry_ref[i * half + j, span] for j in range(half)], axis=0).astype(F32)
            for chip in order:
                out_ref[span * CHIPS + chip, i] = total.astype(BF16)
                total += near_ref[span * CHIPS + chip, i].astype(F32)


def chip_carry(near, carry):
    return pl.pallas_call(
        spread_kernel,
        out_shape=pltpu.VMEM(near.shape, BF16),
        in_specs=[pl.BlockSpec(memory_space=pltpu.VMEM)] * 2,
        out_specs=pl.BlockSpec(memory_space=pltpu.VMEM),
        compiler_params=params(),
        name="chip_carry",
    )(near, carry)


def inner_kernel(core_ref, q_ref, k_ref, v_ref, g_ref, other_ref, out_ref, kept_ref):
    rows = q_ref.shape[0]
    core = core_ref[0]

    def place(axis):
        at = lax.broadcasted_iota(jnp.int32, (2 * rows, 2 * rows), axis)
        return jnp.where(at < rows, at + core * rows, at - core * rows)

    lower = place(0) >= place(1)
    for head in range(STEP_HEADS):
        query, key, value, grad = tokens_of((q_ref, k_ref, v_ref, g_ref), other_ref, head)
        value_scores = jnp.where(lower, dot(grad, value, (1, 1)), 0.0).astype(BF16)
        key_scores = jnp.where(lower, dot(query, key, (1, 1)), 0.0).astype(BF16)
        columns = slice(head * HEAD_DIM, (head + 1) * HEAD_DIM)
        out_ref[0, :, columns] = dot(value_scores, key, (1, 0))
        out_ref[1, :, columns] = dot(value_scores, query, (0, 0))
        out_ref[2, :, columns] = dot(key_scores, grad, (0, 0))
        for i, operand in enumerate((grad, value, key)):
            kept_ref[i, :, columns] = operand


def inner_part(core, arrays, other):
    rows, width = arrays[0].shape
    own_spec, other_spec = token_specs(rows)
    columns = STEP_HEADS * HEAD_DIM
    return pl.pallas_call(
        inner_kernel,
        out_shape=[pltpu.HBM((3, 2 * rows, width // CORES), dtype) for dtype in (F32, BF16)],
        grid_spec=pltpu.PrefetchScalarGridSpec(
            num_scalar_prefetch=1,
            grid=(STEPS,),
            in_specs=[own_spec] * 4 + [other_spec],
            out_specs=[pl.BlockSpec((3, 2 * rows, columns), lambda i, core: (0, 0, i))] * 2,
        ),
        compiler_params=params(LARGE),
        cost_estimate=pl.CostEstimate(
            flops=10 * HALF_HEADS * (2 * rows) ** 2 * HEAD_DIM, bytes_accessed=12 * 2**20, transcendentals=0
        ),
        name="inner_part",
    )(core, *arrays, other)


def outer_part(rows, head, inner_ref, kept_ref, carry_ref):
    columns = slice(head * HEAD_DIM, (head + 1) * HEAD_DIM)
    grad, value, key = [kept_ref[i, rows, columns] for i in range(3)]
    prior, later = read_state(carry_ref, head, 0), read_state(carry_ref, head, 1)
    outer = (dot(grad, prior, (1, 1)), dot(value, later, (1, 1)), dot(key, later, (1, 0)))
    return columns, [(part + inner_ref[i, rows, columns]).astype(BF16) for i, part in enumerate(outer)]


def other_kernel(inner_ref, kept_ref, carry_ref, out_ref):
    rows = out_ref.shape[1]
    for head in range(HALF_HEADS):
        columns, results = outer_part(slice(rows, 2 * rows), head, inner_ref, kept_ref, carry_ref)
        for i, result in enumerate(results):
            out_ref[i, :, columns] = result


def other_gradients(inner, kept, carry):
    _, rows, half = kept.shape
    return pl.pallas_call(
        other_kernel,
        out_shape=pltpu.VMEM((3, rows // 2, half), BF16),
        in_specs=[pl.BlockSpec(memory_space=pltpu.VMEM)] * 3,
        out_specs=pl.BlockSpec(memory_space=pltpu.VMEM),
        compiler_params=params(),
        name="other_gradients",
    )(inner, kept, carry)


def own_kernel(inner_ref, kept_ref, carry_ref, gq_ref, gk_ref, gv_ref, held, sems):
    rows, half = held.shape[1:]
    place = lax.axis_index("core") * half
    copies = []
    for head in range(HALF_HEADS):
        columns, results = outer_part(slice(0, rows), head, inner_ref, kept_ref, carry_ref)
        for i, result in enumerate(results):
            held[i, :, columns] = result
        if (head + 1) % STEP_HEADS == 0:
            width = STEP_HEADS * HEAD_DIM
            first = columns.stop - width
            for i, ref in enumerate((gq_ref, gk_ref, gv_ref)):
                target = ref.at[:, pl.ds(pl.multiple_of(place + first, width), width)]
                copies.append(
                    pltpu.make_async_copy(held.at[i, :, pl.ds(first, width)], target, sems.at[len(copies)])
                )
                copies[-1].start()
    for copy in copies:
        copy.wait()


def own_gradients(inner, kept, carry):
    _, rows, half = kept.shape
    return pl.pallas_call(
        own_kernel,
        out_shape=[pltpu.HBM((rows // 2, half * CORES), BF16)] * 3,
        in_specs=[pl.BlockSpec(memory_space=pltpu.VMEM)] * 3,
        out_specs=[pl.BlockSpec(memory_space=pltpu.HBM)] * 3,
        scratch_shapes=[pltpu.VMEM((3, rows // 2, half), BF16), pltpu.SemaphoreType.DMA((3 * STEPS,))],
        compiler_params=params(),
        cost_estimate=pl.CostEstimate(
            flops=3 * HALF_HEADS * rows * HEAD_DIM**2, bytes_accessed=4 * 2**20, transcendentals=0
        ),
        name="own_gradients",
    )(inner, kept, carry)


def place_kernel(got_ref, q_in, k_in, v_in, gq_ref, gk_ref, gv_ref, sems):
    half = got_ref.shape[2]
    columns = pl.ds(pl.multiple_of((1 - lax.axis_index("core")) * half, half), half)
    copy_all([(got_ref.at[i], ref.at[:, columns]) for i, ref in enumerate((gq_ref, gk_ref, gv_ref))], sems)


def place_half(got, grads):
    any_space = pl.BlockSpec(memory_space=pl.ANY)
    return pl.pallas_call(
        place_kernel,
        out_shape=[jax.ShapeDtypeStruct(array.shape, array.dtype) for array in grads],
        in_specs=[pl.BlockSpec(memory_space=pltpu.VMEM)] + [any_space] * 3,
        out_specs=[any_space] * 3,
        scratch_shapes=[pltpu.SemaphoreType.DMA((3 * got.shape[1] // BAND,))],
        input_output_aliases={1: 0, 2: 1, 3: 2},
        compiler_params=params(),
        name="place_half",
    )(got, *grads)


def exchange(array, axes):
    return lax.all_to_all(array, axes, split_axis=0, concat_axis=0, tiled=True)


def local(queries, keys, values, grad_out):
    arrays = (queries, keys, values, grad_out)
    swap = [(0, 1), (1, 0)]
    core = lax.axis_index("core").reshape(1)
    other = lax.ppermute(pick(arrays, False), "core", swap)
    near = exchange(chunk_states(pick(arrays, True), other), NEAR_AXES)
    near, *inner = lax.optimization_barrier((near, *inner_part(core, arrays, other)))
    far = exchange(group_total(near), FAR_AXES)
    carry = exchange(group_carry(far), FAR_AXES)
    carry = exchange(chip_carry(near, carry), NEAR_AXES)
    got = lax.ppermute(other_gradients(*inner, carry), "core", swap)
    return tuple(place_half(got, own_gradients(*inner, carry)))


def solution(mesh):
    sizes = {"yf": SPANS_Y // NEAR_Y, "yn": NEAR_Y, "zh": FAR_Z, "zl": 2, "x": 4, "core": CORES}
    names = tuple(sizes)
    chips = Mesh(mesh.devices.reshape(tuple(sizes.values())), names)
    rows = P(names, None)
    return jax.shard_map(
        local, mesh=chips, in_specs=(rows,) * 4, out_specs=(rows,) * 3, check_vma=False
    )
```

```python
import functools

import jax
import jax.numpy as jnp
from jax import lax
from jax.experimental import pallas as pl
from jax.experimental.pallas import tpu as pltpu
from jax.sharding import Mesh
from jax.sharding import PartitionSpec as P

HEADS = 32
HEAD_DIM = 128
CORES, SPANS_Y, NEAR_Y, CHIPS, FAR_Z, BLOCK = 2, 4, 4, 8, 8, 16
NEAR, FAR = NEAR_Y * CHIPS, SPANS_Y // NEAR_Y * FAR_Z
HALF_HEADS = HEADS // CORES
OWNED_ROWS = HALF_HEADS * HEAD_DIM // NEAR
STEPS = 4
STEP_HEADS = HALF_HEADS // STEPS
F32, BF16 = jnp.float32, jnp.bfloat16
NEAR_AXES, FAR_AXES = ("zl", "x", "yn"), ("yf", "zh")
BAND = 64
SMALL, LARGE = 32 * 1024 * 1024, 60 * 1024 * 1024


def params(limit=SMALL):
    return pltpu.CompilerParams(vmem_limit_bytes=limit)


def in_hbm(array):
    return pltpu.with_memory_space_constraint(array, pltpu.HBM)


def dot(a, b, contract):
    return lax.dot_general(a, b, (((contract[0],), (contract[1],)), ((), ())), preferred_element_type=F32)


def copy_all(pairs, sems):
    copies = []
    for source, target in pairs:
        for first in range(0, source.shape[0], BAND):
            band = pl.ds(first, BAND)
            copies.append(pltpu.make_async_copy(source.at[band], target.at[band], sems.at[len(copies)]))
    for copy in copies:
        copy.start()
    for copy in copies:
        copy.wait()


def pick_kernel(own, q_ref, k_ref, v_ref, g_ref, out_ref, sems):
    half = out_ref.shape[2]
    core = lax.axis_index("core")
    columns = pl.ds(pl.multiple_of((core if own else 1 - core) * half, half), half)
    copy_all([(ref.at[:, columns], out_ref.at[i]) for i, ref in enumerate((q_ref, k_ref, v_ref, g_ref))], sems)


def pick(arrays, own):
    rows, width = arrays[0].shape
    return pl.pallas_call(
        functools.partial(pick_kernel, own),
        out_shape=pltpu.VMEM((4, rows, width // CORES), BF16),
        in_specs=[pl.BlockSpec(memory_space=pltpu.HBM)] * 4,
        out_specs=pl.BlockSpec(memory_space=pltpu.VMEM),
        scratch_shapes=[pltpu.SemaphoreType.DMA((4 * rows // BAND,))],
        compiler_params=params(),
        cost_estimate=pl.CostEstimate(flops=0, bytes_accessed=2 * 4 * rows * width, transcendentals=0),
        name="own_half" if own else "other_half",
    )(*[in_hbm(array) for array in arrays])


def state_kernel(own_ref, other_ref, out_ref, held, sems):
    copies = []
    for head in range(HALF_HEADS):
        columns = slice(head * HEAD_DIM, (head + 1) * HEAD_DIM)
        query, key, value, grad = [
            jnp.concatenate([own_ref[i, :, columns], other_ref[i, :, columns]], axis=0) for i in range(4)
        ]
        for i, state in enumerate((dot(key, value, (0, 0)), dot(query, grad, (0, 0)))):
            write_state(held, head, i, state.astype(BF16))
        if (head + 1) % 2 == 0:
            share = pl.ds((head - 1) * NEAR // HALF_HEADS, 2 * NEAR // HALF_HEADS)
            copies.append(pltpu.make_async_copy(held.at[share], out_ref.at[share], sems.at[len(copies)]))
            copies[-1].start()
    for copy in copies:
        copy.wait()


def write_state(ref, head, i, state):
    first = head * HEAD_DIM
    for row in range(0, HEAD_DIM, min(HEAD_DIM, OWNED_ROWS)):
        owner, at = divmod(first + row, OWNED_ROWS)
        count = min(HEAD_DIM, OWNED_ROWS)
        ref[owner, i, at : at + count] = state[row : row + count]


def read_state(ref, head, i):
    first, count = head * HEAD_DIM, min(HEAD_DIM, OWNED_ROWS)
    parts = []
    for row in range(0, HEAD_DIM, count):
        owner, at = divmod(first + row, OWNED_ROWS)
        parts.append(ref[owner, i, at : at + count])
    return parts[0] if len(parts) == 1 else jnp.concatenate(parts, axis=0)


def chunk_states(own, other):
    shape = (NEAR, 2, OWNED_ROWS, HEAD_DIM)
    return pl.pallas_call(
        state_kernel,
        out_shape=pltpu.HBM(shape, BF16),
        in_specs=[pl.BlockSpec(memory_space=pltpu.VMEM)] * 2,
        out_specs=pl.BlockSpec(memory_space=pltpu.HBM),
        scratch_shapes=[pltpu.VMEM(shape, BF16), pltpu.SemaphoreType.DMA((HALF_HEADS // 2,))],
        compiler_params=params(),
        name="chunk_states",
    )(own, other)


def tokens_of(refs, other_ref, head):
    columns = slice(head * HEAD_DIM, (head + 1) * HEAD_DIM)
    return [
        jnp.concatenate([ref[:, columns], other_ref[i, :, columns]], axis=0) for i, ref in enumerate(refs)
    ]


def token_specs(rows):
    columns = STEP_HEADS * HEAD_DIM
    own = pl.BlockSpec((rows, columns), lambda i, core: (0, core[0] * STEPS + i))
    other = pl.BlockSpec((4, rows, columns), lambda i, core: (0, 0, i))
    return own, other


def member(span, chip):
    place = {"yn": span, "zl": chip // 4, "x": chip % 4}
    sizes = {"yn": NEAR_Y, "zl": 2, "x": 4}
    index = 0
    for axis in NEAR_AXES:
        index = index * sizes[axis] + place[axis]
    return index


def total_kernel(near_ref, out_ref):
    half = FAR // 2
    for span in range(NEAR_Y):
        total = near_ref[member(span, 0)].astype(F32)
        for chip in range(1, CHIPS):
            total += near_ref[member(span, chip)].astype(F32)
        total = total.astype(BF16)
        for slot in range(FAR):
            block = slot % half * BLOCK
            out_ref[slot, span] = total[slot // half, block : block + BLOCK]


def group_total(near):
    return pl.pallas_call(
        total_kernel,
        out_shape=pltpu.VMEM((FAR, NEAR_Y, BLOCK, HEAD_DIM), BF16),
        in_specs=[pl.BlockSpec(memory_space=pltpu.VMEM)],
        out_specs=pl.BlockSpec(memory_space=pltpu.VMEM),
        compiler_params=params(),
        name="group_total",
    )(near)


def groups_in_order():
    order = []
    for y in range(SPANS_Y):
        far_at, near_at = divmod(y, NEAR_Y)
        order += [(far_at * FAR_Z + z, near_at) for z in range(FAR_Z)]
    return order


def carry_kernel(far_ref, out_ref):
    place = lax.axis_index(FAR_AXES)

    def run(order):
        total = jnp.zeros((BLOCK, HEAD_DIM), F32)
        for group in order:
            out_ref[group] = total.astype(BF16)
            total += far_ref[group].astype(F32)

    @pl.when(place < FAR // 2)
    def _():
        run(groups_in_order())

    @pl.when(place >= FAR // 2)
    def _():
        run(groups_in_order()[::-1])


def group_carry(far):
    return pl.pallas_call(
        carry_kernel,
        out_shape=pltpu.VMEM(far.shape, BF16),
        in_specs=[pl.BlockSpec(memory_space=pltpu.VMEM)],
        out_specs=pl.BlockSpec(memory_space=pltpu.VMEM),
        compiler_params=params(),
        name="group_carry",
    )(far)


def spread_kernel(near_ref, carry_ref, out_ref):
    half = FAR // 2
    for span in range(NEAR_Y):
        for i, order in enumerate((range(CHIPS), range(CHIPS)[::-1])):
            total = jnp.concatenate([carry_ref[i * half + j, span] for j in range(half)], axis=0).astype(F32)
            for chip in order:
                out_ref[member(span, chip), i] = total.astype(BF16)
                total += near_ref[member(span, chip), i].astype(F32)


def chip_carry(near, carry):
    return pl.pallas_call(
        spread_kernel,
        out_shape=pltpu.VMEM(near.shape, BF16),
        in_specs=[pl.BlockSpec(memory_space=pltpu.VMEM)] * 2,
        out_specs=pl.BlockSpec(memory_space=pltpu.VMEM),
        compiler_params=params(),
        name="chip_carry",
    )(near, carry)


def inner_kernel(core_ref, q_ref, k_ref, v_ref, g_ref, other_ref, out_ref, kept_ref):
    rows = q_ref.shape[0]
    core = core_ref[0]

    def place(axis):
        at = lax.broadcasted_iota(jnp.int32, (2 * rows, 2 * rows), axis)
        return jnp.where(at < rows, at + core * rows, at - core * rows)

    lower = place(0) >= place(1)
    for head in range(STEP_HEADS):
        query, key, value, grad = tokens_of((q_ref, k_ref, v_ref, g_ref), other_ref, head)
        value_scores = jnp.where(lower, dot(grad, value, (1, 1)), 0.0).astype(BF16)
        key_scores = jnp.where(lower, dot(query, key, (1, 1)), 0.0).astype(BF16)
        columns = slice(head * HEAD_DIM, (head + 1) * HEAD_DIM)
        out_ref[0, :, columns] = dot(value_scores, key, (1, 0))
        out_ref[1, :, columns] = dot(value_scores, query, (0, 0))
        out_ref[2, :, columns] = dot(key_scores, grad, (0, 0))
        for i, operand in enumerate((grad, value, key)):
            kept_ref[i, :, columns] = operand


def inner_part(core, arrays, other):
    rows, width = arrays[0].shape
    own_spec, other_spec = token_specs(rows)
    columns = STEP_HEADS * HEAD_DIM
    return pl.pallas_call(
        inner_kernel,
        out_shape=[pltpu.HBM((3, 2 * rows, width // CORES), dtype) for dtype in (F32, BF16)],
        grid_spec=pltpu.PrefetchScalarGridSpec(
            num_scalar_prefetch=1,
            grid=(STEPS,),
            in_specs=[own_spec] * 4 + [other_spec],
            out_specs=[pl.BlockSpec((3, 2 * rows, columns), lambda i, core: (0, 0, i))] * 2,
        ),
        compiler_params=params(LARGE),
        cost_estimate=pl.CostEstimate(
            flops=10 * HALF_HEADS * (2 * rows) ** 2 * HEAD_DIM, bytes_accessed=12 * 2**20, transcendentals=0
        ),
        name="inner_part",
    )(core, *arrays, other)


def outer_part(rows, head, inner_ref, kept_ref, carry_ref):
    columns = slice(head * HEAD_DIM, (head + 1) * HEAD_DIM)
    grad, value, key = [kept_ref[i, rows, columns] for i in range(3)]
    prior, later = read_state(carry_ref, head, 0), read_state(carry_ref, head, 1)
    outer = (dot(grad, prior, (1, 1)), dot(value, later, (1, 1)), dot(key, later, (1, 0)))
    return columns, [(part + inner_ref[i, rows, columns]).astype(BF16) for i, part in enumerate(outer)]


def other_kernel(inner_ref, kept_ref, carry_ref, out_ref):
    rows = out_ref.shape[1]
    for head in range(HALF_HEADS):
        columns, results = outer_part(slice(rows, 2 * rows), head, inner_ref, kept_ref, carry_ref)
        for i, result in enumerate(results):
            out_ref[i, :, columns] = result


def other_gradients(inner, kept, carry):
    _, rows, half = kept.shape
    return pl.pallas_call(
        other_kernel,
        out_shape=pltpu.VMEM((3, rows // 2, half), BF16),
        in_specs=[pl.BlockSpec(memory_space=pltpu.VMEM)] * 3,
        out_specs=pl.BlockSpec(memory_space=pltpu.VMEM),
        compiler_params=params(),
        name="other_gradients",
    )(inner, kept, carry)


def own_kernel(inner_ref, kept_ref, carry_ref, gq_ref, gk_ref, gv_ref, held, sems):
    rows, half = held.shape[1:]
    place = lax.axis_index("core") * half
    copies = []
    for head in range(HALF_HEADS):
        columns, results = outer_part(slice(0, rows), head, inner_ref, kept_ref, carry_ref)
        for i, result in enumerate(results):
            held[i, :, columns] = result
        if (head + 1) % STEP_HEADS == 0:
            width = STEP_HEADS * HEAD_DIM
            first = columns.stop - width
            for i, ref in enumerate((gq_ref, gk_ref, gv_ref)):
                target = ref.at[:, pl.ds(pl.multiple_of(place + first, width), width)]
                copies.append(
                    pltpu.make_async_copy(held.at[i, :, pl.ds(first, width)], target, sems.at[len(copies)])
                )
                copies[-1].start()
    for copy in copies:
        copy.wait()


def own_gradients(inner, kept, carry):
    _, rows, half = kept.shape
    return pl.pallas_call(
        own_kernel,
        out_shape=[pltpu.HBM((rows // 2, half * CORES), BF16)] * 3,
        in_specs=[pl.BlockSpec(memory_space=pltpu.VMEM)] * 3,
        out_specs=[pl.BlockSpec(memory_space=pltpu.HBM)] * 3,
        scratch_shapes=[pltpu.VMEM((3, rows // 2, half), BF16), pltpu.SemaphoreType.DMA((3 * STEPS,))],
        compiler_params=params(),
        cost_estimate=pl.CostEstimate(
            flops=3 * HALF_HEADS * rows * HEAD_DIM**2, bytes_accessed=4 * 2**20, transcendentals=0
        ),
        name="own_gradients",
    )(inner, kept, carry)


def place_kernel(got_ref, q_in, k_in, v_in, gq_ref, gk_ref, gv_ref, sems):
    half = got_ref.shape[2]
    columns = pl.ds(pl.multiple_of((1 - lax.axis_index("core")) * half, half), half)
    copy_all([(got_ref.at[i], ref.at[:, columns]) for i, ref in enumerate((gq_ref, gk_ref, gv_ref))], sems)


def place_half(got, grads):
    any_space = pl.BlockSpec(memory_space=pl.ANY)
    return pl.pallas_call(
        place_kernel,
        out_shape=[jax.ShapeDtypeStruct(array.shape, array.dtype) for array in grads],
        in_specs=[pl.BlockSpec(memory_space=pltpu.VMEM)] + [any_space] * 3,
        out_specs=[any_space] * 3,
        scratch_shapes=[pltpu.SemaphoreType.DMA((3 * got.shape[1] // BAND,))],
        input_output_aliases={1: 0, 2: 1, 3: 2},
        compiler_params=params(),
        name="place_half",
    )(got, *grads)


def exchange(array, axes):
    return lax.all_to_all(array, axes, split_axis=0, concat_axis=0, tiled=True)


def local(queries, keys, values, grad_out):
    arrays = (queries, keys, values, grad_out)
    swap = [(0, 1), (1, 0)]
    core = lax.axis_index("core").reshape(1)
    other = lax.ppermute(pick(arrays, False), "core", swap)
    near = exchange(chunk_states(pick(arrays, True), other), NEAR_AXES)
    near, *inner = lax.optimization_barrier((near, *inner_part(core, arrays, other)))
    far = exchange(group_total(near), FAR_AXES)
    carry = exchange(group_carry(far), FAR_AXES)
    carry = exchange(chip_carry(near, carry), NEAR_AXES)
    got = lax.ppermute(other_gradients(*inner, carry), "core", swap)
    return tuple(place_half(got, own_gradients(*inner, carry)))


def solution(mesh):
    sizes = {"yf": SPANS_Y // NEAR_Y, "yn": NEAR_Y, "zh": FAR_Z, "zl": 2, "x": 4, "core": CORES}
    names = tuple(sizes)
    chips = Mesh(mesh.devices.reshape(tuple(sizes.values())), names)
    rows = P(names, None)
    return jax.shard_map(
        local, mesh=chips, in_specs=(rows,) * 4, out_specs=(rows,) * 3, check_vma=False
    )
```

```python
import functools

import jax
import jax.numpy as jnp
from jax import lax
from jax.experimental import pallas as pl
from jax.experimental.pallas import tpu as pltpu
from jax.sharding import Mesh
from jax.sharding import PartitionSpec as P

HEADS = 32
HEAD_DIM = 128
CORES, SPANS_Y, NEAR_Y, CHIPS, FAR_Z, BLOCK = 2, 4, 4, 8, 8, 16
NEAR, FAR = NEAR_Y * CHIPS, SPANS_Y // NEAR_Y * FAR_Z
HALF_HEADS = HEADS // CORES
OWNED_ROWS = HALF_HEADS * HEAD_DIM // NEAR
STEPS = 4
STEP_HEADS = HALF_HEADS // STEPS
F32, BF16 = jnp.float32, jnp.bfloat16
NEAR_AXES, FAR_AXES = ("zl", "x", "yn"), ("yf", "zc", "zb", "za")
BAND = 64
SMALL, LARGE = 32 * 1024 * 1024, 60 * 1024 * 1024


def params(limit=SMALL):
    return pltpu.CompilerParams(vmem_limit_bytes=limit)


def in_hbm(array):
    return pltpu.with_memory_space_constraint(array, pltpu.HBM)


def dot(a, b, contract):
    return lax.dot_general(a, b, (((contract[0],), (contract[1],)), ((), ())), preferred_element_type=F32)


def copy_all(pairs, sems):
    copies = []
    for source, target in pairs:
        for first in range(0, source.shape[0], BAND):
            band = pl.ds(first, BAND)
            copies.append(pltpu.make_async_copy(source.at[band], target.at[band], sems.at[len(copies)]))
    for copy in copies:
        copy.start()
    for copy in copies:
        copy.wait()


def pick_kernel(own, q_ref, k_ref, v_ref, g_ref, out_ref, sems):
    half = out_ref.shape[2]
    core = lax.axis_index("core")
    columns = pl.ds(pl.multiple_of((core if own else 1 - core) * half, half), half)
    copy_all([(ref.at[:, columns], out_ref.at[i]) for i, ref in enumerate((q_ref, k_ref, v_ref, g_ref))], sems)


def pick(arrays, own):
    rows, width = arrays[0].shape
    return pl.pallas_call(
        functools.partial(pick_kernel, own),
        out_shape=pltpu.VMEM((4, rows, width // CORES), BF16),
        in_specs=[pl.BlockSpec(memory_space=pltpu.HBM)] * 4,
        out_specs=pl.BlockSpec(memory_space=pltpu.VMEM),
        scratch_shapes=[pltpu.SemaphoreType.DMA((4 * rows // BAND,))],
        compiler_params=params(),
        cost_estimate=pl.CostEstimate(flops=0, bytes_accessed=2 * 4 * rows * width, transcendentals=0),
        name="own_half" if own else "other_half",
    )(*[in_hbm(array) for array in arrays])


def state_kernel(own_ref, other_ref, out_ref, held, sems):
    copies = []
    for head in range(HALF_HEADS):
        columns = slice(head * HEAD_DIM, (head + 1) * HEAD_DIM)
        query, key, value, grad = [
            jnp.concatenate([own_ref[i, :, columns], other_ref[i, :, columns]], axis=0) for i in range(4)
        ]
        for i, state in enumerate((dot(key, value, (0, 0)), dot(query, grad, (0, 0)))):
            write_state(held, head, i, state.astype(BF16))
        if (head + 1) % 2 == 0:
            share = pl.ds((head - 1) * NEAR // HALF_HEADS, 2 * NEAR // HALF_HEADS)
            copies.append(pltpu.make_async_copy(held.at[share], out_ref.at[share], sems.at[len(copies)]))
            copies[-1].start()
    for copy in copies:
        copy.wait()


def write_state(ref, head, i, state):
    first = head * HEAD_DIM
    for row in range(0, HEAD_DIM, min(HEAD_DIM, OWNED_ROWS)):
        owner, at = divmod(first + row, OWNED_ROWS)
        count = min(HEAD_DIM, OWNED_ROWS)
        ref[owner, i, at : at + count] = state[row : row + count]


def read_state(ref, head, i):
    first, count = head * HEAD_DIM, min(HEAD_DIM, OWNED_ROWS)
    parts = []
    for row in range(0, HEAD_DIM, count):
        owner, at = divmod(first + row, OWNED_ROWS)
        parts.append(ref[owner, i, at : at + count])
    return parts[0] if len(parts) == 1 else jnp.concatenate(parts, axis=0)


def chunk_states(own, other):
    shape = (NEAR, 2, OWNED_ROWS, HEAD_DIM)
    return pl.pallas_call(
        state_kernel,
        out_shape=pltpu.HBM(shape, BF16),
        in_specs=[pl.BlockSpec(memory_space=pltpu.VMEM)] * 2,
        out_specs=pl.BlockSpec(memory_space=pltpu.HBM),
        scratch_shapes=[pltpu.VMEM(shape, BF16), pltpu.SemaphoreType.DMA((HALF_HEADS // 2,))],
        compiler_params=params(),
        name="chunk_states",
    )(own, other)


def tokens_of(refs, other_ref, head):
    columns = slice(head * HEAD_DIM, (head + 1) * HEAD_DIM)
    return [
        jnp.concatenate([ref[:, columns], other_ref[i, :, columns]], axis=0) for i, ref in enumerate(refs)
    ]


def token_specs(rows):
    columns = STEP_HEADS * HEAD_DIM
    own = pl.BlockSpec((rows, columns), lambda i, core: (0, core[0] * STEPS + i))
    other = pl.BlockSpec((4, rows, columns), lambda i, core: (0, 0, i))
    return own, other


def member(span, chip):
    place = {"yn": span, "zl": chip // 4, "x": chip % 4}
    sizes = {"yn": NEAR_Y, "zl": 2, "x": 4}
    index = 0
    for axis in NEAR_AXES:
        index = index * sizes[axis] + place[axis]
    return index


def total_kernel(near_ref, out_ref):
    half = FAR // 2
    for span in range(NEAR_Y):
        total = near_ref[member(span, 0)].astype(F32)
        for chip in range(1, CHIPS):
            total += near_ref[member(span, chip)].astype(F32)
        total = total.astype(BF16)
        for slot in range(FAR):
            block = slot % half * BLOCK
            out_ref[slot, span] = total[slot // half, block : block + BLOCK]


def group_total(near):
    return pl.pallas_call(
        total_kernel,
        out_shape=pltpu.VMEM((FAR, NEAR_Y, BLOCK, HEAD_DIM), BF16),
        in_specs=[pl.BlockSpec(memory_space=pltpu.VMEM)],
        out_specs=pl.BlockSpec(memory_space=pltpu.VMEM),
        compiler_params=params(),
        name="group_total",
    )(near)


def groups_in_order():
    order = []
    for y in range(SPANS_Y):
        far_at, near_at = divmod(y, NEAR_Y)
        order += [(far_at * FAR_Z + z % 2 * 4 + z // 2 % 2 * 2 + z // 4, near_at) for z in range(FAR_Z)]
    return order


def carry_kernel(far_ref, out_ref):
    place = lax.axis_index(FAR_AXES)

    def run(order):
        total = jnp.zeros((BLOCK, HEAD_DIM), F32)
        for group in order:
            out_ref[group] = total.astype(BF16)
            total += far_ref[group].astype(F32)

    @pl.when(place < FAR // 2)
    def _():
        run(groups_in_order())

    @pl.when(place >= FAR // 2)
    def _():
        run(groups_in_order()[::-1])


def group_carry(far):
    return pl.pallas_call(
        carry_kernel,
        out_shape=pltpu.VMEM(far.shape, BF16),
        in_specs=[pl.BlockSpec(memory_space=pltpu.VMEM)],
        out_specs=pl.BlockSpec(memory_space=pltpu.VMEM),
        compiler_params=params(),
        name="group_carry",
    )(far)


def spread_kernel(near_ref, carry_ref, out_ref):
    half = FAR // 2
    for span in range(NEAR_Y):
        for i, order in enumerate((range(CHIPS), range(CHIPS)[::-1])):
            total = jnp.concatenate([carry_ref[i * half + j, span] for j in range(half)], axis=0).astype(F32)
            for chip in order:
                out_ref[member(span, chip), i] = total.astype(BF16)
                total += near_ref[member(span, chip), i].astype(F32)


def chip_carry(near, carry):
    return pl.pallas_call(
        spread_kernel,
        out_shape=pltpu.VMEM(near.shape, BF16),
        in_specs=[pl.BlockSpec(memory_space=pltpu.VMEM)] * 2,
        out_specs=pl.BlockSpec(memory_space=pltpu.VMEM),
        compiler_params=params(),
        name="chip_carry",
    )(near, carry)


def inner_kernel(core_ref, q_ref, k_ref, v_ref, g_ref, other_ref, out_ref, kept_ref):
    rows = q_ref.shape[0]
    core = core_ref[0]

    def place(axis):
        at = lax.broadcasted_iota(jnp.int32, (2 * rows, 2 * rows), axis)
        return jnp.where(at < rows, at + core * rows, at - core * rows)

    lower = place(0) >= place(1)
    for head in range(STEP_HEADS):
        query, key, value, grad = tokens_of((q_ref, k_ref, v_ref, g_ref), other_ref, head)
        value_scores = jnp.where(lower, dot(grad, value, (1, 1)), 0.0).astype(BF16)
        key_scores = jnp.where(lower, dot(query, key, (1, 1)), 0.0).astype(BF16)
        columns = slice(head * HEAD_DIM, (head + 1) * HEAD_DIM)
        out_ref[0, :, columns] = dot(value_scores, key, (1, 0))
        out_ref[1, :, columns] = dot(value_scores, query, (0, 0))
        out_ref[2, :, columns] = dot(key_scores, grad, (0, 0))
        for i, operand in enumerate((grad, value, key)):
            kept_ref[i, :, columns] = operand


def inner_part(core, arrays, other):
    rows, width = arrays[0].shape
    own_spec, other_spec = token_specs(rows)
    columns = STEP_HEADS * HEAD_DIM
    return pl.pallas_call(
        inner_kernel,
        out_shape=[pltpu.HBM((3, 2 * rows, width // CORES), dtype) for dtype in (F32, BF16)],
        grid_spec=pltpu.PrefetchScalarGridSpec(
            num_scalar_prefetch=1,
            grid=(STEPS,),
            in_specs=[own_spec] * 4 + [other_spec],
            out_specs=[pl.BlockSpec((3, 2 * rows, columns), lambda i, core: (0, 0, i))] * 2,
        ),
        compiler_params=params(LARGE),
        cost_estimate=pl.CostEstimate(
            flops=10 * HALF_HEADS * (2 * rows) ** 2 * HEAD_DIM, bytes_accessed=12 * 2**20, transcendentals=0
        ),
        name="inner_part",
    )(core, *arrays, other)


def outer_part(rows, head, inner_ref, kept_ref, carry_ref):
    columns = slice(head * HEAD_DIM, (head + 1) * HEAD_DIM)
    grad, value, key = [kept_ref[i, rows, columns] for i in range(3)]
    prior, later = read_state(carry_ref, head, 0), read_state(carry_ref, head, 1)
    outer = (dot(grad, prior, (1, 1)), dot(value, later, (1, 1)), dot(key, later, (1, 0)))
    return columns, [(part + inner_ref[i, rows, columns]).astype(BF16) for i, part in enumerate(outer)]


def other_kernel(inner_ref, kept_ref, carry_ref, out_ref):
    rows = out_ref.shape[1]
    for head in range(HALF_HEADS):
        columns, results = outer_part(slice(rows, 2 * rows), head, inner_ref, kept_ref, carry_ref)
        for i, result in enumerate(results):
            out_ref[i, :, columns] = result


def other_gradients(inner, kept, carry):
    _, rows, half = kept.shape
    return pl.pallas_call(
        other_kernel,
        out_shape=pltpu.VMEM((3, rows // 2, half), BF16),
        in_specs=[pl.BlockSpec(memory_space=pltpu.VMEM)] * 3,
        out_specs=pl.BlockSpec(memory_space=pltpu.VMEM),
        compiler_params=params(),
        name="other_gradients",
    )(inner, kept, carry)


def own_kernel(inner_ref, kept_ref, carry_ref, gq_ref, gk_ref, gv_ref, held, sems):
    rows, half = held.shape[1:]
    place = lax.axis_index("core") * half
    copies = []
    for head in range(HALF_HEADS):
        columns, results = outer_part(slice(0, rows), head, inner_ref, kept_ref, carry_ref)
        for i, result in enumerate(results):
            held[i, :, columns] = result
        if (head + 1) % STEP_HEADS == 0:
            width = STEP_HEADS * HEAD_DIM
            first = columns.stop - width
            for i, ref in enumerate((gq_ref, gk_ref, gv_ref)):
                target = ref.at[:, pl.ds(pl.multiple_of(place + first, width), width)]
                copies.append(
                    pltpu.make_async_copy(held.at[i, :, pl.ds(first, width)], target, sems.at[len(copies)])
                )
                copies[-1].start()
    for copy in copies:
        copy.wait()


def own_gradients(inner, kept, carry):
    _, rows, half = kept.shape
    return pl.pallas_call(
        own_kernel,
        out_shape=[pltpu.HBM((rows // 2, half * CORES), BF16)] * 3,
        in_specs=[pl.BlockSpec(memory_space=pltpu.VMEM)] * 3,
        out_specs=[pl.BlockSpec(memory_space=pltpu.HBM)] * 3,
        scratch_shapes=[pltpu.VMEM((3, rows // 2, half), BF16), pltpu.SemaphoreType.DMA((3 * STEPS,))],
        compiler_params=params(),
        cost_estimate=pl.CostEstimate(
            flops=3 * HALF_HEADS * rows * HEAD_DIM**2, bytes_accessed=4 * 2**20, transcendentals=0
        ),
        name="own_gradients",
    )(inner, kept, carry)


def place_kernel(got_ref, q_in, k_in, v_in, gq_ref, gk_ref, gv_ref, sems):
    half = got_ref.shape[2]
    columns = pl.ds(pl.multiple_of((1 - lax.axis_index("core")) * half, half), half)
    copy_all([(got_ref.at[i], ref.at[:, columns]) for i, ref in enumerate((gq_ref, gk_ref, gv_ref))], sems)


def place_half(got, grads):
    any_space = pl.BlockSpec(memory_space=pl.ANY)
    return pl.pallas_call(
        place_kernel,
        out_shape=[jax.ShapeDtypeStruct(array.shape, array.dtype) for array in grads],
        in_specs=[pl.BlockSpec(memory_space=pltpu.VMEM)] + [any_space] * 3,
        out_specs=[any_space] * 3,
        scratch_shapes=[pltpu.SemaphoreType.DMA((3 * got.shape[1] // BAND,))],
        input_output_aliases={1: 0, 2: 1, 3: 2},
        compiler_params=params(),
        name="place_half",
    )(got, *grads)


def exchange(array, axes):
    return lax.all_to_all(array, axes, split_axis=0, concat_axis=0, tiled=True)


def local(queries, keys, values, grad_out):
    arrays = (queries, keys, values, grad_out)
    swap = [(0, 1), (1, 0)]
    core = lax.axis_index("core").reshape(1)
    other = lax.ppermute(pick(arrays, False), "core", swap)
    near = exchange(chunk_states(pick(arrays, True), other), NEAR_AXES)
    near, *inner = lax.optimization_barrier((near, *inner_part(core, arrays, other)))
    far = exchange(group_total(near), FAR_AXES)
    carry = exchange(group_carry(far), FAR_AXES)
    carry = exchange(chip_carry(near, carry), NEAR_AXES)
    got = lax.ppermute(other_gradients(*inner, carry), "core", swap)
    return tuple(place_half(got, own_gradients(*inner, carry)))


def solution(mesh):
    sizes = {"yf": SPANS_Y // NEAR_Y, "yn": NEAR_Y, "za": 2, "zb": 2, "zc": 2, "zl": 2, "x": 4, "core": CORES}
    names = tuple(sizes)
    chips = Mesh(mesh.devices.reshape(tuple(sizes.values())), names)
    rows = P(names, None)
    return jax.shard_map(
        local, mesh=chips, in_specs=(rows,) * 4, out_specs=(rows,) * 3, check_vma=False
    )
```

```python
import functools

import jax
import jax.numpy as jnp
from jax import lax
from jax.experimental import pallas as pl
from jax.experimental.pallas import tpu as pltpu
from jax.sharding import Mesh
from jax.sharding import PartitionSpec as P

HEADS = 32
HEAD_DIM = 128
CORES, SPANS_Y, NEAR_Y, CHIPS, FAR_Z, BLOCK = 2, 4, 4, 8, 8, 16
NEAR, FAR = NEAR_Y * CHIPS, SPANS_Y // NEAR_Y * FAR_Z
HALF_HEADS = HEADS // CORES
OWNED_ROWS = HALF_HEADS * HEAD_DIM // NEAR
STEPS = 4
STEP_HEADS = HALF_HEADS // STEPS
F32, BF16 = jnp.float32, jnp.bfloat16
NEAR_AXES, FAR_AXES = ("zl", "x", "yl", "yh"), ("yf", "zc", "zb", "za")
BAND = 64
SMALL, LARGE = 32 * 1024 * 1024, 60 * 1024 * 1024


def params(limit=SMALL):
    return pltpu.CompilerParams(vmem_limit_bytes=limit)


def in_hbm(array):
    return pltpu.with_memory_space_constraint(array, pltpu.HBM)


def dot(a, b, contract):
    return lax.dot_general(a, b, (((contract[0],), (contract[1],)), ((), ())), preferred_element_type=F32)


def copy_all(pairs, sems):
    copies = []
    for source, target in pairs:
        for first in range(0, source.shape[0], BAND):
            band = pl.ds(first, BAND)
            copies.append(pltpu.make_async_copy(source.at[band], target.at[band], sems.at[len(copies)]))
    for copy in copies:
        copy.start()
    for copy in copies:
        copy.wait()


def pick_kernel(own, q_ref, k_ref, v_ref, g_ref, out_ref, sems):
    half = out_ref.shape[2]
    core = lax.axis_index("core")
    columns = pl.ds(pl.multiple_of((core if own else 1 - core) * half, half), half)
    copy_all([(ref.at[:, columns], out_ref.at[i]) for i, ref in enumerate((q_ref, k_ref, v_ref, g_ref))], sems)


def pick(arrays, own):
    rows, width = arrays[0].shape
    return pl.pallas_call(
        functools.partial(pick_kernel, own),
        out_shape=pltpu.VMEM((4, rows, width // CORES), BF16),
        in_specs=[pl.BlockSpec(memory_space=pltpu.HBM)] * 4,
        out_specs=pl.BlockSpec(memory_space=pltpu.VMEM),
        scratch_shapes=[pltpu.SemaphoreType.DMA((4 * rows // BAND,))],
        compiler_params=params(),
        cost_estimate=pl.CostEstimate(flops=0, bytes_accessed=2 * 4 * rows * width, transcendentals=0),
        name="own_half" if own else "other_half",
    )(*[in_hbm(array) for array in arrays])


def state_kernel(own_ref, other_ref, out_ref, held, sems):
    copies = []
    for head in range(HALF_HEADS):
        columns = slice(head * HEAD_DIM, (head + 1) * HEAD_DIM)
        query, key, value, grad = [
            jnp.concatenate([own_ref[i, :, columns], other_ref[i, :, columns]], axis=0) for i in range(4)
        ]
        for i, state in enumerate((dot(key, value, (0, 0)), dot(query, grad, (0, 0)))):
            write_state(held, head, i, state.astype(BF16))
        if (head + 1) % 2 == 0:
            share = pl.ds((head - 1) * NEAR // HALF_HEADS, 2 * NEAR // HALF_HEADS)
            copies.append(pltpu.make_async_copy(held.at[share], out_ref.at[share], sems.at[len(copies)]))
            copies[-1].start()
    for copy in copies:
        copy.wait()


def write_state(ref, head, i, state):
    first = head * HEAD_DIM
    for row in range(0, HEAD_DIM, min(HEAD_DIM, OWNED_ROWS)):
        owner, at = divmod(first + row, OWNED_ROWS)
        count = min(HEAD_DIM, OWNED_ROWS)
        ref[owner, i, at : at + count] = state[row : row + count]


def read_state(ref, head, i):
    first, count = head * HEAD_DIM, min(HEAD_DIM, OWNED_ROWS)
    parts = []
    for row in range(0, HEAD_DIM, count):
        owner, at = divmod(first + row, OWNED_ROWS)
        parts.append(ref[owner, i, at : at + count])
    return parts[0] if len(parts) == 1 else jnp.concatenate(parts, axis=0)


def chunk_states(own, other):
    shape = (NEAR, 2, OWNED_ROWS, HEAD_DIM)
    return pl.pallas_call(
        state_kernel,
        out_shape=pltpu.HBM(shape, BF16),
        in_specs=[pl.BlockSpec(memory_space=pltpu.VMEM)] * 2,
        out_specs=pl.BlockSpec(memory_space=pltpu.HBM),
        scratch_shapes=[pltpu.VMEM(shape, BF16), pltpu.SemaphoreType.DMA((HALF_HEADS // 2,))],
        compiler_params=params(),
        name="chunk_states",
    )(own, other)


def tokens_of(refs, other_ref, head):
    columns = slice(head * HEAD_DIM, (head + 1) * HEAD_DIM)
    return [
        jnp.concatenate([ref[:, columns], other_ref[i, :, columns]], axis=0) for i, ref in enumerate(refs)
    ]


def token_specs(rows):
    columns = STEP_HEADS * HEAD_DIM
    own = pl.BlockSpec((rows, columns), lambda i, core: (0, core[0] * STEPS + i))
    other = pl.BlockSpec((4, rows, columns), lambda i, core: (0, 0, i))
    return own, other


def member(span, chip):
    place = {"yh": span // 2, "yl": span % 2, "zl": chip // 4, "x": chip % 4}
    sizes = {"yh": 2, "yl": 2, "zl": 2, "x": 4}
    index = 0
    for axis in NEAR_AXES:
        index = index * sizes[axis] + place[axis]
    return index


def total_kernel(near_ref, out_ref):
    half = FAR // 2
    for span in range(NEAR_Y):
        total = near_ref[member(span, 0)].astype(F32)
        for chip in range(1, CHIPS):
            total += near_ref[member(span, chip)].astype(F32)
        total = total.astype(BF16)
        for slot in range(FAR):
            block = slot % half * BLOCK
            out_ref[slot, span] = total[slot // half, block : block + BLOCK]


def group_total(near):
    return pl.pallas_call(
        total_kernel,
        out_shape=pltpu.VMEM((FAR, NEAR_Y, BLOCK, HEAD_DIM), BF16),
        in_specs=[pl.BlockSpec(memory_space=pltpu.VMEM)],
        out_specs=pl.BlockSpec(memory_space=pltpu.VMEM),
        compiler_params=params(),
        name="group_total",
    )(near)


def groups_in_order():
    order = []
    for y in range(SPANS_Y):
        far_at, near_at = divmod(y, NEAR_Y)
        order += [(far_at * FAR_Z + z % 2 * 4 + z // 2 % 2 * 2 + z // 4, near_at) for z in range(FAR_Z)]
    return order


def carry_kernel(far_ref, out_ref):
    place = lax.axis_index(FAR_AXES)

    def run(order):
        total = jnp.zeros((BLOCK, HEAD_DIM), F32)
        for group in order:
            out_ref[group] = total.astype(BF16)
            total += far_ref[group].astype(F32)

    @pl.when(place < FAR // 2)
    def _():
        run(groups_in_order())

    @pl.when(place >= FAR // 2)
    def _():
        run(groups_in_order()[::-1])


def group_carry(far):
    return pl.pallas_call(
        carry_kernel,
        out_shape=pltpu.VMEM(far.shape, BF16),
        in_specs=[pl.BlockSpec(memory_space=pltpu.VMEM)],
        out_specs=pl.BlockSpec(memory_space=pltpu.VMEM),
        compiler_params=params(),
        name="group_carry",
    )(far)


def spread_kernel(near_ref, carry_ref, out_ref):
    half = FAR // 2
    for span in range(NEAR_Y):
        for i, order in enumerate((range(CHIPS), range(CHIPS)[::-1])):
            total = jnp.concatenate([carry_ref[i * half + j, span] for j in range(half)], axis=0).astype(F32)
            for chip in order:
                out_ref[member(span, chip), i] = total.astype(BF16)
                total += near_ref[member(span, chip), i].astype(F32)


def chip_carry(near, carry):
    return pl.pallas_call(
        spread_kernel,
        out_shape=pltpu.VMEM(near.shape, BF16),
        in_specs=[pl.BlockSpec(memory_space=pltpu.VMEM)] * 2,
        out_specs=pl.BlockSpec(memory_space=pltpu.VMEM),
        compiler_params=params(),
        name="chip_carry",
    )(near, carry)


def inner_kernel(core_ref, q_ref, k_ref, v_ref, g_ref, other_ref, out_ref, kept_ref):
    rows = q_ref.shape[0]
    core = core_ref[0]

    def place(axis):
        at = lax.broadcasted_iota(jnp.int32, (2 * rows, 2 * rows), axis)
        return jnp.where(at < rows, at + core * rows, at - core * rows)

    lower = place(0) >= place(1)
    for head in range(STEP_HEADS):
        query, key, value, grad = tokens_of((q_ref, k_ref, v_ref, g_ref), other_ref, head)
        value_scores = jnp.where(lower, dot(grad, value, (1, 1)), 0.0).astype(BF16)
        key_scores = jnp.where(lower, dot(query, key, (1, 1)), 0.0).astype(BF16)
        columns = slice(head * HEAD_DIM, (head + 1) * HEAD_DIM)
        out_ref[0, :, columns] = dot(value_scores, key, (1, 0))
        out_ref[1, :, columns] = dot(value_scores, query, (0, 0))
        out_ref[2, :, columns] = dot(key_scores, grad, (0, 0))
        for i, operand in enumerate((grad, value, key)):
            kept_ref[i, :, columns] = operand


def inner_part(core, arrays, other):
    rows, width = arrays[0].shape
    own_spec, other_spec = token_specs(rows)
    columns = STEP_HEADS * HEAD_DIM
    return pl.pallas_call(
        inner_kernel,
        out_shape=[pltpu.HBM((3, 2 * rows, width // CORES), dtype) for dtype in (F32, BF16)],
        grid_spec=pltpu.PrefetchScalarGridSpec(
            num_scalar_prefetch=1,
            grid=(STEPS,),
            in_specs=[own_spec] * 4 + [other_spec],
            out_specs=[pl.BlockSpec((3, 2 * rows, columns), lambda i, core: (0, 0, i))] * 2,
        ),
        compiler_params=params(LARGE),
        cost_estimate=pl.CostEstimate(
            flops=10 * HALF_HEADS * (2 * rows) ** 2 * HEAD_DIM, bytes_accessed=12 * 2**20, transcendentals=0
        ),
        name="inner_part",
    )(core, *arrays, other)


def outer_part(rows, head, inner_ref, kept_ref, carry_ref):
    columns = slice(head * HEAD_DIM, (head + 1) * HEAD_DIM)
    grad, value, key = [kept_ref[i, rows, columns] for i in range(3)]
    prior, later = read_state(carry_ref, head, 0), read_state(carry_ref, head, 1)
    outer = (dot(grad, prior, (1, 1)), dot(value, later, (1, 1)), dot(key, later, (1, 0)))
    return columns, [(part + inner_ref[i, rows, columns]).astype(BF16) for i, part in enumerate(outer)]


def other_kernel(inner_ref, kept_ref, carry_ref, out_ref):
    rows = out_ref.shape[1]
    for head in range(HALF_HEADS):
        columns, results = outer_part(slice(rows, 2 * rows), head, inner_ref, kept_ref, carry_ref)
        for i, result in enumerate(results):
            out_ref[i, :, columns] = result


def other_gradients(inner, kept, carry):
    _, rows, half = kept.shape
    return pl.pallas_call(
        other_kernel,
        out_shape=pltpu.VMEM((3, rows // 2, half), BF16),
        in_specs=[pl.BlockSpec(memory_space=pltpu.VMEM)] * 3,
        out_specs=pl.BlockSpec(memory_space=pltpu.VMEM),
        compiler_params=params(),
        name="other_gradients",
    )(inner, kept, carry)


def own_kernel(inner_ref, kept_ref, carry_ref, gq_ref, gk_ref, gv_ref, held, sems):
    rows, half = held.shape[1:]
    place = lax.axis_index("core") * half
    copies = []
    for head in range(HALF_HEADS):
        columns, results = outer_part(slice(0, rows), head, inner_ref, kept_ref, carry_ref)
        for i, result in enumerate(results):
            held[i, :, columns] = result
        if (head + 1) % STEP_HEADS == 0:
            width = STEP_HEADS * HEAD_DIM
            first = columns.stop - width
            for i, ref in enumerate((gq_ref, gk_ref, gv_ref)):
                target = ref.at[:, pl.ds(pl.multiple_of(place + first, width), width)]
                copies.append(
                    pltpu.make_async_copy(held.at[i, :, pl.ds(first, width)], target, sems.at[len(copies)])
                )
                copies[-1].start()
    for copy in copies:
        copy.wait()


def own_gradients(inner, kept, carry):
    _, rows, half = kept.shape
    return pl.pallas_call(
        own_kernel,
        out_shape=[pltpu.HBM((rows // 2, half * CORES), BF16)] * 3,
        in_specs=[pl.BlockSpec(memory_space=pltpu.VMEM)] * 3,
        out_specs=[pl.BlockSpec(memory_space=pltpu.HBM)] * 3,
        scratch_shapes=[pltpu.VMEM((3, rows // 2, half), BF16), pltpu.SemaphoreType.DMA((3 * STEPS,))],
        compiler_params=params(),
        cost_estimate=pl.CostEstimate(
            flops=3 * HALF_HEADS * rows * HEAD_DIM**2, bytes_accessed=4 * 2**20, transcendentals=0
        ),
        name="own_gradients",
    )(inner, kept, carry)


def place_kernel(got_ref, q_in, k_in, v_in, gq_ref, gk_ref, gv_ref, sems):
    half = got_ref.shape[2]
    columns = pl.ds(pl.multiple_of((1 - lax.axis_index("core")) * half, half), half)
    copy_all([(got_ref.at[i], ref.at[:, columns]) for i, ref in enumerate((gq_ref, gk_ref, gv_ref))], sems)


def place_half(got, grads):
    any_space = pl.BlockSpec(memory_space=pl.ANY)
    return pl.pallas_call(
        place_kernel,
        out_shape=[jax.ShapeDtypeStruct(array.shape, array.dtype) for array in grads],
        in_specs=[pl.BlockSpec(memory_space=pltpu.VMEM)] + [any_space] * 3,
        out_specs=[any_space] * 3,
        scratch_shapes=[pltpu.SemaphoreType.DMA((3 * got.shape[1] // BAND,))],
        input_output_aliases={1: 0, 2: 1, 3: 2},
        compiler_params=params(),
        name="place_half",
    )(got, *grads)


def exchange(array, axes):
    return lax.all_to_all(array, axes, split_axis=0, concat_axis=0, tiled=True)


def local(queries, keys, values, grad_out):
    arrays = (queries, keys, values, grad_out)
    swap = [(0, 1), (1, 0)]
    core = lax.axis_index("core").reshape(1)
    other = lax.ppermute(pick(arrays, False), "core", swap)
    near = exchange(chunk_states(pick(arrays, True), other), NEAR_AXES)
    near, *inner = lax.optimization_barrier((near, *inner_part(core, arrays, other)))
    far = exchange(group_total(near), FAR_AXES)
    carry = exchange(group_carry(far), FAR_AXES)
    carry = exchange(chip_carry(near, carry), NEAR_AXES)
    got = lax.ppermute(other_gradients(*inner, carry), "core", swap)
    return tuple(place_half(got, own_gradients(*inner, carry)))


def solution(mesh):
    sizes = {"yf": SPANS_Y // NEAR_Y, "yh": 2, "yl": 2, "za": 2, "zb": 2, "zc": 2, "zl": 2, "x": 4, "core": CORES}
    names = tuple(sizes)
    chips = Mesh(mesh.devices.reshape(tuple(sizes.values())), names)
    rows = P(names, None)
    return jax.shard_map(
        local, mesh=chips, in_specs=(rows,) * 4, out_specs=(rows,) * 3, check_vma=False
    )
```
